32 devices in a mesh: fish: 2 (over y), img: 16 (over z, x, core).
Axes of the slice: x: 2, y: 2, z: 4, core: 2. Of those that a mesh axis runs over, the one named last changes fastest.
Arguments:
- img_feat: bfloat16 [64, 16384], P(None, ('fish', 'img')), parts along dimension 1, may hold values from -80 to 80
- mdl_feat: bfloat16 [64, 2048], P(None, ('fish', 'img')), parts along dimension 1, may hold values from -80 to 80
- img_mass: float32 [16384], P(('fish', 'img')), parts along dimension 0, may hold values from 0.5 to 2
- mdl_mass: float32 [2048], P('fish'), parts along dimension 0, may hold values from 0.5 to 2
Outputs:
- grad_img: float32 [64, 16384], P(None, ('fish', 'img')), parts along dimension 1
- grad_mdl: float32 [64, 2048], P(None, ('fish', 'img')), parts along dimension 1
The draws below stay inside these ranges and needn't reach their ends.
There are 2 independent parts, one for each index of `fish`. The reference program is written for one: setup_inputs(seed, part) draws one part's arguments, and reference() takes and returns one part's arrays. A program takes and returns all parts, laid end to end along the dimension named above; each array names one. Nothing has to cross between parts.
All inputs are finite; a program needn't handle non-finite values.
Results may differ from the reference program's by a relative error of at most 0.005.
Values may be sent and summed in bfloat16 or wider, within the bound.
A program may use at most 64 MiB of HBM per device.

```python
import math
import jax
import jax.numpy as jnp
from jax import lax

FEAT = 64
ROWS_DEV = 512
ITERS = 4
IMAGED = 8192
MODEL = 1024


def paired_features(key):
    base_key, perm_key, noise_key, img_scale_key, mdl_scale_key = jax.random.split(jax.random.fold_in(key, 11), 5)
    base = jnp.clip(jax.random.normal(base_key, (FEAT, IMAGED), jnp.float32), -4.0, 4.0)
    noise = 0.8 * jnp.clip(jax.random.normal(noise_key, (FEAT, MODEL), jnp.float32), -4.0, 4.0)
    chosen = jax.random.permutation(perm_key, IMAGED)[:MODEL]
    matched = base[:, chosen] + noise
    img_scale = jnp.exp(jax.random.uniform(img_scale_key, (1, IMAGED), jnp.float32, 0.0, 2.3))
    mdl_scale = jnp.exp(jax.random.uniform(mdl_scale_key, (1, MODEL), jnp.float32, 0.0, 2.3))
    return (base * img_scale, matched * mdl_scale)


def draw_img_feat(key, part):
    return paired_features(key)[0].astype(jnp.bfloat16)


def draw_mdl_feat(key, part):
    return paired_features(key)[1].astype(jnp.bfloat16)


def steps_of(stream_key, extent, cuts, least, top_value):
    def one(position, parts):
        heights = jax.random.uniform(jax.random.fold_in(jax.random.fold_in(stream_key, 6), position), (parts,), jnp.float32, least / len(cuts), top_value / len(cuts))
        return jnp.repeat(jnp.exp(heights), extent[position] // parts).reshape((-1,) + (1,) * (len(extent) - position - 1))

    loudness = one(*cuts[0])
    for cut in cuts[1:]:
        loudness = loudness * one(*cut)
    return loudness


def setup_inputs(seed: int = 0, part: int = 0) -> dict:
    streams_of = jax.random.split(jax.random.key(seed), 5)
    part_splits = jax.random.split(jax.random.fold_in(streams_of[4], part), 5)
    img_feat = draw_img_feat(jax.random.fold_in(jax.random.fold_in(streams_of[4], part), 71), part)
    mdl_feat = draw_mdl_feat(jax.random.fold_in(jax.random.fold_in(streams_of[4], part), 71), part)
    img_mass = jnp.clip(jnp.exp(math.log(2.0) - 1.3862944 * jax.random.uniform(part_splits[2], (IMAGED,), jnp.float32) ** steps_of(part_splits[2], (IMAGED,), ((0, 16),), -0.2, 0.2)), 0.5, 2.0)
    mdl_mass = jnp.clip(jnp.exp(jax.random.uniform(part_splits[3], (MODEL,), jnp.float32, math.log(0.5), math.log(2.0))), 0.5, 2.0)
    return {"img_feat": img_feat, "mdl_feat": mdl_feat, "img_mass": img_mass, "mdl_mass": mdl_mass}


inv_temp = 20.0

def normalize(features):
    wide = features.astype(jnp.float32)
    guarded = lax.optimization_barrier(jnp.mean(wide * wide, axis=0, keepdims=True)) + 1e-06
    return (wide * lax.rsqrt(guarded)).astype(jnp.bfloat16)

def reference(img_feat, mdl_feat, img_mass, mdl_mass):
    factor = inv_temp / FEAT
    imaged_unit = normalize(img_feat)
    model_unit = normalize(mdl_feat)
    nblocks = IMAGED // ROWS_DEV
    model_wide = model_unit.astype(jnp.float32)
    row_blocks = imaged_unit.reshape(FEAT, nblocks, ROWS_DEV).transpose(1, 0, 2)

    def build(unit_block):
        scores = jnp.dot(unit_block.astype(jnp.float32).T, model_wide)
        return jnp.exp(scores * factor).astype(jnp.bfloat16)
    kernel = lax.map(build, row_blocks)
    col_scale = jnp.ones((MODEL,), jnp.float32)
    col_low = col_scale.astype(jnp.bfloat16)
    row_scale = jnp.ones((IMAGED,), jnp.float32)
    for iteration in range(ITERS):
        low_wide = col_low.astype(jnp.float32)
        row_sums = lax.map(lambda tile_block: jnp.dot(tile_block.astype(jnp.float32), low_wide), kernel)
        row_scale = img_mass / row_sums.reshape(IMAGED)
        row_low = row_scale.astype(jnp.bfloat16).astype(jnp.float32).reshape(nblocks, ROWS_DEV)

        def add_cols(carry, pair):
            tile_block, low_block = pair
            return (carry + jnp.dot(low_block, tile_block.astype(jnp.float32)), None)
        col_sum, unused = lax.scan(add_cols, jnp.zeros((MODEL,), jnp.float32), (kernel, row_low))
        col_scale = mdl_mass / col_sum
        col_low = col_scale.astype(jnp.bfloat16)
    weighted = (model_wide * col_scale[None, :]).astype(jnp.bfloat16).astype(jnp.float32)
    image_terms = lax.map(lambda tile_block: jnp.dot(weighted, tile_block.astype(jnp.float32).T), kernel)
    image_terms = image_terms.transpose(1, 0, 2).reshape(FEAT, IMAGED)
    grad_img = -(image_terms * row_scale[None, :])
    row_feat = (imaged_unit.astype(jnp.float32) * row_scale[None, :]).astype(jnp.bfloat16).astype(jnp.float32)
    feat_blocks = row_feat.reshape(FEAT, nblocks, ROWS_DEV).transpose(1, 0, 2)

    def add_model(carry, pair):
        tile_block, feat_block = pair
        return (carry + jnp.dot(tile_block.astype(jnp.float32).T, feat_block.T), None)
    model_terms, unused = lax.scan(add_model, jnp.zeros((MODEL, FEAT), jnp.float32), (kernel, feat_blocks))
    grad_mdl = -(model_terms.T * col_scale[None, :])
    return (grad_img, grad_mdl)
```

```python
import functools

import jax
import jax.numpy as jnp
from jax import lax
from jax.experimental import pallas as pl
from jax.experimental.pallas import tpu as pltpu
from jax.sharding import PartitionSpec as P

FEAT = 64
ITERS = 4
LANES = 128
HALF = 64
REP = 16

inv_temp = 20.0


def normalize(features):
    wide = features.astype(jnp.float32)
    guarded = jnp.mean(wide * wide, axis=0, keepdims=True) + 1e-06
    return wide * lax.rsqrt(guarded)


def repeat(count, body):
    if count <= 16:
        for step in range(count):
            body(step)
    else:
        lax.fori_loop(0, count, lambda step, carry: (body(step), carry)[1], 0)


def whole_kernel(
    n, img_ref, mdl_ref, img_mass_ref, mdl_mass_ref, grad_img_ref, grad_mdl_ref,
    units, model, kern, parts, scale, feat_out, feat_in, send_sem, recv_sem,
):
    me = lax.axis_index("img")
    total = kern.shape[1]
    lines = total // LANES

    def partner(step):
        return lax.rem(me + step + 1, n)

    def send(phase, source, target_slot):
        def one(step):
            to = partner(step)
            pltpu.make_async_remote_copy(
                src_ref=source(to),
                dst_ref=target_slot,
                send_sem=send_sem.at[phase],
                recv_sem=recv_sem.at[phase],
                device_id={"img": to},
                device_id_type=pl.DeviceIdType.MESH,
            ).start()

        repeat(n - 1, one)

    def arrived(phase, slots):
        all_but_own = slots.at[pl.ds(0, n - 1)]
        pltpu.make_async_copy(all_but_own, all_but_own, recv_sem.at[phase]).wait()

    def sent(phase, slots):
        all_but_own = slots.at[pl.ds(0, n - 1)]
        pltpu.make_async_copy(all_but_own, all_but_own, send_sem.at[phase]).wait()

    barrier = pltpu.get_barrier_semaphore()

    def greet(step):
        pl.semaphore_signal(
            barrier, inc=1, device_id={"img": partner(step)}, device_id_type=pl.DeviceIdType.MESH
        )

    repeat(n - 1, greet)

    own = normalize(mdl_ref[...])
    units[me] = jnp.concatenate([own[: FEAT // 2], own[FEAT // 2 :]], axis=1).astype(jnp.bfloat16)
    pl.semaphore_wait(barrier, n - 1)
    send(0, lambda to: units.at[me], units.at[me])

    img_unit = normalize(img_ref[...]).astype(jnp.bfloat16)
    img_rows = img_unit.astype(jnp.float32).T.astype(jnp.bfloat16)
    img_mass = img_mass_ref[...]
    left = lax.broadcasted_iota(jnp.int32, (FEAT // 2, LANES), 1) < HALF

    arrived(0, units)

    factor = inv_temp / FEAT
    chunk = 2 * LANES

    def build(step):
        blocks = []
        for sub in range(chunk // LANES):
            pair = step * (chunk // LANES) + sub
            one = units[2 * pair].astype(jnp.float32)
            two = units[2 * pair + 1].astype(jnp.float32)
            top = jnp.where(left, one, pltpu.roll(two, HALF, 1))
            bottom = jnp.where(left, pltpu.roll(one, HALF, 1), two)
            blocks.append(jnp.concatenate([top, bottom], axis=0))
        columns = jnp.concatenate(blocks, axis=1).astype(jnp.bfloat16)
        where = pl.ds(step * chunk if isinstance(step, int) else pl.multiple_of(step * chunk, chunk), chunk)
        model[:, where] = columns
        scores = jnp.dot(img_rows, columns, preferred_element_type=jnp.float32)
        kern[:, where] = jnp.exp(scores * factor).astype(jnp.bfloat16)

    repeat(total // chunk, build)

    col_wide = jnp.ones((REP, total), jnp.float32)
    for iteration in range(ITERS):
        row_sums = lax.dot_general(
            col_wide.astype(jnp.bfloat16), kern[...], (((1,), (1,)), ((), ())),
            preferred_element_type=jnp.float32,
        )
        row_scale = img_mass / row_sums
        partial_cols = jnp.dot(
            row_scale.astype(jnp.bfloat16), kern[...], preferred_element_type=jnp.float32
        )
        for line in range(lines):
            parts[iteration, me, line : line + 1, :] = partial_cols[:1, line * LANES : (line + 1) * LANES]
        send(1 + iteration, lambda to: parts.at[iteration, me], parts.at[iteration, me])

        if iteration == ITERS - 1:
            row_feat = (img_unit.astype(jnp.float32) * row_scale[:1]).astype(jnp.bfloat16)
            for pair in range(n // 2):
                both = jnp.dot(
                    row_feat, kern[:, pair * LANES : (pair + 1) * LANES],
                    preferred_element_type=jnp.float32,
                )
                top, bottom = both[: FEAT // 2], both[FEAT // 2 :]
                feat_out[2 * pair] = jnp.where(left, top, pltpu.roll(bottom, HALF, 1)).astype(jnp.bfloat16)
                feat_out[2 * pair + 1] = jnp.where(left, pltpu.roll(top, HALF, 1), bottom).astype(jnp.bfloat16)
            send(1 + ITERS, lambda to: feat_out.at[to], feat_in.at[me])

        arrived(1 + iteration, parts.at[iteration])
        col_sum = jnp.sum(parts[iteration], axis=0)
        scale[...] = mdl_mass_ref[...] / col_sum
        col_wide = jnp.concatenate(
            [jnp.broadcast_to(scale[line : line + 1, :], (REP, LANES)) for line in range(lines)], axis=1
        )

    weighted = (model[...].astype(jnp.float32) * col_wide[:1]).astype(jnp.bfloat16)
    image_terms = lax.dot_general(
        weighted, kern[...], (((1,), (1,)), ((), ())), preferred_element_type=jnp.float32
    )
    grad_img_ref[...] = -(image_terms * row_scale[:1])

    feat_in[me] = feat_out[me]
    arrived(1 + ITERS, feat_in)
    summed = jnp.sum(feat_in[...].astype(jnp.float32), axis=0)
    line = scale[pl.ds(me // 2, 1), :]
    even = lax.rem(me, 2) == 0
    own_scale = jnp.where(left[:1] == even, line, pltpu.roll(line, HALF, 1))
    packed = -(summed * own_scale)
    grad_mdl_ref[: FEAT // 2] = packed[:, :HALF]
    grad_mdl_ref[FEAT // 2 :] = pltpu.roll(packed, HALF, 1)[:, :HALF]

    sent(0, units)
    for iteration in range(ITERS):
        sent(1 + iteration, parts.at[iteration])
    sent(1 + ITERS, feat_out)


def shards(n, img_feat, mdl_feat, img_mass, mdl_mass):
    rows = img_feat.shape[1]
    share = mdl_feat.shape[1]
    total = share * n
    assert share == HALF and img_feat.shape[0] == FEAT
    lines = total // LANES
    vmem = pl.BlockSpec(memory_space=pltpu.VMEM)
    packed = (n, FEAT // 2, LANES)
    return pl.pallas_call(
        functools.partial(whole_kernel, n),
        out_shape=(
            jax.ShapeDtypeStruct((FEAT, rows), jnp.float32),
            jax.ShapeDtypeStruct((FEAT, share), jnp.float32),
        ),
        in_specs=[vmem] * 4,
        out_specs=(vmem, vmem),
        scratch_shapes=[
            pltpu.VMEM(packed, jnp.bfloat16),
            pltpu.VMEM((FEAT, total), jnp.bfloat16),
            pltpu.VMEM((rows, total), jnp.bfloat16),
            pltpu.VMEM((ITERS, n, lines, LANES), jnp.float32),
            pltpu.VMEM((lines, LANES), jnp.float32),
            pltpu.VMEM(packed, jnp.bfloat16),
            pltpu.VMEM(packed, jnp.bfloat16),
            pltpu.SemaphoreType.DMA((2 + ITERS,)),
            pltpu.SemaphoreType.DMA((2 + ITERS,)),
        ],
        compiler_params=pltpu.CompilerParams(
            collective_id=0, has_side_effects=True, vmem_limit_bytes=56 * 2**20
        ),
        name="sinkhorn",
    )(img_feat, mdl_feat, img_mass.reshape(1, rows), mdl_mass.reshape(lines, LANES))


def solution(mesh):
    placed = (P(None, ("fish", "img")), P(None, ("fish", "img")), P(("fish", "img")), P("fish"))
    return jax.shard_map(
        functools.partial(shards, mesh.shape["img"]),
        mesh=mesh,
        in_specs=placed,
        out_specs=(P(None, ("fish", "img")), P(None, ("fish", "img"))),
        check_vma=False,
    )
```

```python
import functools

import jax
import jax.numpy as jnp
from jax import lax
from jax.experimental import pallas as pl
from jax.experimental.pallas import tpu as pltpu
from jax.sharding import PartitionSpec as P

FEAT = 64
ITERS = 4
LANES = 128
HALF = 64
REP = 16

inv_temp = 20.0


def normalize(features):
    wide = features.astype(jnp.float32)
    guarded = jnp.mean(wide * wide, axis=0, keepdims=True) + 1e-06
    return wide * lax.rsqrt(guarded)


def repeat(count, body):
    if count <= 16:
        for step in range(count):
            body(step)
    else:
        lax.fori_loop(0, count, lambda step, carry: (body(step), carry)[1], 0)


def whole_kernel(
    n, img_hbm, mdl_hbm, img_mass_hbm, mdl_mass_hbm, grad_img_ref, grad_mdl_ref,
    img_ref, mdl_ref, img_mass_ref, mdl_mass_ref,
    units, model, kern, parts, scale, feat_out, feat_in, load_sem, send_sem, recv_sem,
):
    me = lax.axis_index("img")
    total = kern.shape[1]
    lines = total // LANES

    def partner(step):
        return lax.rem(me + step + 1, n)

    def send(phase, source, target_slot):
        def one(step):
            to = partner(step)
            pltpu.make_async_remote_copy(
                src_ref=source(to),
                dst_ref=target_slot,
                send_sem=send_sem.at[phase],
                recv_sem=recv_sem.at[phase],
                device_id={"img": to},
                device_id_type=pl.DeviceIdType.MESH,
            ).start()

        repeat(n - 1, one)

    def arrived(phase, slots):
        all_but_own = slots.at[pl.ds(0, n - 1)]
        pltpu.make_async_copy(all_but_own, all_but_own, recv_sem.at[phase]).wait()

    def sent(phase, slots):
        all_but_own = slots.at[pl.ds(0, n - 1)]
        pltpu.make_async_copy(all_but_own, all_but_own, send_sem.at[phase]).wait()

    barrier = pltpu.get_barrier_semaphore()

    def greet(step):
        pl.semaphore_signal(
            barrier, inc=1, device_id={"img": partner(step)}, device_id_type=pl.DeviceIdType.MESH
        )

    loads = [
        pltpu.make_async_copy(source, target, load_sem.at[slot])
        for slot, (source, target) in enumerate(
            ((mdl_hbm, mdl_ref), (img_hbm, img_ref), (img_mass_hbm, img_mass_ref), (mdl_mass_hbm, mdl_mass_ref))
        )
    ]
    for load in loads:
        load.start()
    repeat(n - 1, greet)
    loads[0].wait()

    own = normalize(mdl_ref[...])
    units[me] = jnp.concatenate([own[: FEAT // 2], own[FEAT // 2 :]], axis=1).astype(jnp.bfloat16)
    pl.semaphore_wait(barrier, n - 1)
    send(0, lambda to: units.at[me], units.at[me])

    for load in loads[1:]:
        load.wait()
    img_unit = normalize(img_ref[...]).astype(jnp.bfloat16)
    img_rows = img_unit.astype(jnp.float32).T.astype(jnp.bfloat16)
    img_mass = img_mass_ref[...]
    left = lax.broadcasted_iota(jnp.int32, (FEAT // 2, LANES), 1) < HALF

    arrived(0, units)

    factor = inv_temp / FEAT
    chunk = 2 * LANES

    def build(step):
        blocks = []
        for sub in range(chunk // LANES):
            pair = step * (chunk // LANES) + sub
            one = units[2 * pair].astype(jnp.float32)
            two = units[2 * pair + 1].astype(jnp.float32)
            top = jnp.where(left, one, pltpu.roll(two, HALF, 1))
            bottom = jnp.where(left, pltpu.roll(one, HALF, 1), two)
            blocks.append(jnp.concatenate([top, bottom], axis=0))
        columns = jnp.concatenate(blocks, axis=1).astype(jnp.bfloat16)
        where = pl.ds(step * chunk if isinstance(step, int) else pl.multiple_of(step * chunk, chunk), chunk)
        model[:, where] = columns
        scores = jnp.dot(img_rows, columns, preferred_element_type=jnp.float32)
        kern[:, where] = jnp.exp(scores * factor).astype(jnp.bfloat16)

    repeat(total // chunk, build)

    col_wide = jnp.ones((REP, total), jnp.float32)
    for iteration in range(ITERS):
        row_sums = lax.dot_general(
            col_wide.astype(jnp.bfloat16), kern[...], (((1,), (1,)), ((), ())),
            preferred_element_type=jnp.float32,
        )
        row_scale = img_mass / row_sums
        partial_cols = jnp.dot(
            row_scale.astype(jnp.bfloat16), kern[...], preferred_element_type=jnp.float32
        )
        for line in range(lines):
            parts[iteration, me, line : line + 1, :] = partial_cols[:1, line * LANES : (line + 1) * LANES]
        send(1 + iteration, lambda to: parts.at[iteration, me], parts.at[iteration, me])

        if iteration == ITERS - 1:
            row_feat = (img_unit.astype(jnp.float32) * row_scale[:1]).astype(jnp.bfloat16)
            for pair in range(n // 2):
                both = jnp.dot(
                    row_feat, kern[:, pair * LANES : (pair + 1) * LANES],
                    preferred_element_type=jnp.float32,
                )
                top, bottom = both[: FEAT // 2], both[FEAT // 2 :]
                feat_out[2 * pair] = jnp.where(left, top, pltpu.roll(bottom, HALF, 1)).astype(jnp.bfloat16)
                feat_out[2 * pair + 1] = jnp.where(left, pltpu.roll(top, HALF, 1), bottom).astype(jnp.bfloat16)
            send(1 + ITERS, lambda to: feat_out.at[to], feat_in.at[me])

        arrived(1 + iteration, parts.at[iteration])
        col_sum = jnp.sum(parts[iteration], axis=0)
        scale[...] = mdl_mass_ref[...] / col_sum
        col_wide = jnp.concatenate(
            [jnp.broadcast_to(scale[line : line + 1, :], (REP, LANES)) for line in range(lines)], axis=1
        )

    weighted = (model[...].astype(jnp.float32) * col_wide[:1]).astype(jnp.bfloat16)
    image_terms = lax.dot_general(
        weighted, kern[...], (((1,), (1,)), ((), ())), preferred_element_type=jnp.float32
    )
    grad_img_ref[...] = -(image_terms * row_scale[:1])

    feat_in[me] = feat_out[me]
    arrived(1 + ITERS, feat_in)
    summed = jnp.sum(feat_in[...].astype(jnp.float32), axis=0)
    line = scale[pl.ds(me // 2, 1), :]
    even = lax.rem(me, 2) == 0
    own_scale = jnp.where(left[:1] == even, line, pltpu.roll(line, HALF, 1))
    packed = -(summed * own_scale)
    grad_mdl_ref[: FEAT // 2] = packed[:, :HALF]
    grad_mdl_ref[FEAT // 2 :] = pltpu.roll(packed, HALF, 1)[:, :HALF]

    sent(0, units)
    for iteration in range(ITERS):
        sent(1 + iteration, parts.at[iteration])
    sent(1 + ITERS, feat_out)


def store_kernel(grad_img_ref, grad_mdl_ref, grad_img_hbm, grad_mdl_hbm, sems):
    stores = [
        pltpu.make_async_copy(grad_img_ref, grad_img_hbm, sems.at[0]),
        pltpu.make_async_copy(grad_mdl_ref, grad_mdl_hbm, sems.at[1]),
    ]
    for store in stores:
        store.start()
    for store in stores:
        store.wait()


def shards(n, img_feat, mdl_feat, img_mass, mdl_mass):
    rows = img_feat.shape[1]
    share = mdl_feat.shape[1]
    total = share * n
    assert share == HALF and img_feat.shape[0] == FEAT
    lines = total // LANES
    vmem = pl.BlockSpec(memory_space=pltpu.VMEM)
    packed = (n, FEAT // 2, LANES)
    anywhere = pl.BlockSpec(memory_space=pl.ANY)
    grads = pl.pallas_call(
        functools.partial(whole_kernel, n),
        out_shape=(
            pltpu.VMEM((FEAT, rows), jnp.float32),
            pltpu.VMEM((FEAT, share), jnp.float32),
        ),
        in_specs=[pl.BlockSpec(memory_space=pltpu.HBM)] * 4,
        out_specs=(vmem, vmem),
        scratch_shapes=[
            pltpu.VMEM((FEAT, rows), jnp.bfloat16),
            pltpu.VMEM((FEAT, share), jnp.bfloat16),
            pltpu.VMEM((1, rows), jnp.float32),
            pltpu.VMEM((lines, LANES), jnp.float32),
            pltpu.VMEM(packed, jnp.bfloat16),
            pltpu.VMEM((FEAT, total), jnp.bfloat16),
            pltpu.VMEM((rows, total), jnp.bfloat16),
            pltpu.VMEM((ITERS, n, lines, LANES), jnp.float32),
            pltpu.VMEM((lines, LANES), jnp.float32),
            pltpu.VMEM(packed, jnp.bfloat16),
            pltpu.VMEM(packed, jnp.bfloat16),
            pltpu.SemaphoreType.DMA((4,)),
            pltpu.SemaphoreType.DMA((2 + ITERS,)),
            pltpu.SemaphoreType.DMA((2 + ITERS,)),
        ],
        compiler_params=pltpu.CompilerParams(
            collective_id=0, has_side_effects=True, vmem_limit_bytes=60 * 2**20
        ),
        name="sinkhorn",
    )(img_feat, mdl_feat, img_mass.reshape(1, rows), mdl_mass.reshape(lines, LANES))
    return pl.pallas_call(
        store_kernel,
        out_shape=(
            jax.ShapeDtypeStruct((FEAT, rows), jnp.float32),
            jax.ShapeDtypeStruct((FEAT, share), jnp.float32),
        ),
        in_specs=[vmem] * 2,
        out_specs=(anywhere, anywhere),
        scratch_shapes=[pltpu.SemaphoreType.DMA((2,))],
        name="store",
    )(*grads)


def solution(mesh):
    placed = (P(None, ("fish", "img")), P(None, ("fish", "img")), P(("fish", "img")), P("fish"))
    return jax.shard_map(
        functools.partial(shards, mesh.shape["img"]),
        mesh=mesh,
        in_specs=placed,
        out_specs=(P(None, ("fish", "img")), P(None, ("fish", "img"))),
        check_vma=False,
    )
```

```python
import functools

import jax
import jax.numpy as jnp
from jax import lax
from jax.experimental import pallas as pl
from jax.experimental.pallas import tpu as pltpu
from jax.sharding import PartitionSpec as P

FEAT = 64
ITERS = 4
LANES = 128
HALF = 64
REP = 16

inv_temp = 20.0


def normalize(features):
    wide = features.astype(jnp.float32)
    guarded = jnp.mean(wide * wide, axis=0, keepdims=True) + 1e-06
    return wide * lax.rsqrt(guarded)


def repeat(count, body):
    if count <= 16:
        for step in range(count):
            body(step)
    else:
        lax.fori_loop(0, count, lambda step, carry: (body(step), carry)[1], 0)


def near_group(n):
    size = 1
    while (2 * size) ** 2 <= n and n % (2 * size) == 0:
        size *= 2
    return size


def whole_kernel(
    n, img_hbm, mdl_hbm, img_mass_hbm, mdl_mass_hbm, grad_img_ref, grad_mdl_ref,
    img_ref, mdl_ref, img_mass_ref, mdl_mass_ref,
    units, model, kern, parts, sums, scale, feat_out, feat_in, load_sem, send_sem, recv_sem,
):
    me = lax.axis_index("img")
    total = kern.shape[1]
    lines = total // LANES

    inner = near_group(n)
    outer = n // inner
    my_inner, my_outer = lax.rem(me, inner), me // inner

    def partner(step):
        return lax.rem(me + step + 1, n)

    def near(step):
        return my_outer * inner + lax.rem(my_inner + step + 1, inner)

    def far(step):
        return lax.rem(my_outer + step + 1, outer) * inner + my_inner

    def send(phase, count, whom, source, target_slot):
        def one(step):
            to = whom(step)
            pltpu.make_async_remote_copy(
                src_ref=source(to),
                dst_ref=target_slot,
                send_sem=send_sem.at[phase],
                recv_sem=recv_sem.at[phase],
                device_id={"img": to},
                device_id_type=pl.DeviceIdType.MESH,
            ).start()

        repeat(count - 1, one)

    def arrived(phase, count, slots):
        all_but_own = slots.at[pl.ds(0, count - 1)]
        pltpu.make_async_copy(all_but_own, all_but_own, recv_sem.at[phase]).wait()

    def sent(phase, count, slots):
        all_but_own = slots.at[pl.ds(0, count - 1)]
        pltpu.make_async_copy(all_but_own, all_but_own, send_sem.at[phase]).wait()

    barrier = pltpu.get_barrier_semaphore()

    def greet(step):
        pl.semaphore_signal(
            barrier, inc=1, device_id={"img": partner(step)}, device_id_type=pl.DeviceIdType.MESH
        )

    loads = [
        pltpu.make_async_copy(source, target, load_sem.at[slot])
        for slot, (source, target) in enumerate(
            ((mdl_hbm, mdl_ref), (img_hbm, img_ref), (img_mass_hbm, img_mass_ref), (mdl_mass_hbm, mdl_mass_ref))
        )
    ]
    for load in loads:
        load.start()
    repeat(n - 1, greet)
    loads[0].wait()

    own = normalize(mdl_ref[...])
    units[me] = jnp.concatenate([own[: FEAT // 2], own[FEAT // 2 :]], axis=1).astype(jnp.bfloat16)
    pl.semaphore_wait(barrier, n - 1)
    send(0, n, partner, lambda to: units.at[me], units.at[me])

    for load in loads[1:]:
        load.wait()
    img_unit = normalize(img_ref[...]).astype(jnp.bfloat16)
    img_rows = img_unit.astype(jnp.float32).T.astype(jnp.bfloat16)
    img_mass = img_mass_ref[...]
    left = lax.broadcasted_iota(jnp.int32, (FEAT // 2, LANES), 1) < HALF

    arrived(0, n, units)

    factor = inv_temp / FEAT
    chunk = 2 * LANES

    def build(step):
        blocks = []
        for sub in range(chunk // LANES):
            pair = step * (chunk // LANES) + sub
            one = units[2 * pair].astype(jnp.float32)
            two = units[2 * pair + 1].astype(jnp.float32)
            top = jnp.where(left, one, pltpu.roll(two, HALF, 1))
            bottom = jnp.where(left, pltpu.roll(one, HALF, 1), two)
            blocks.append(jnp.concatenate([top, bottom], axis=0))
        columns = jnp.concatenate(blocks, axis=1).astype(jnp.bfloat16)
        where = pl.ds(step * chunk if isinstance(step, int) else pl.multiple_of(step * chunk, chunk), chunk)
        model[:, where] = columns
        scores = jnp.dot(img_rows, columns, preferred_element_type=jnp.float32)
        kern[:, where] = jnp.exp(scores * factor).astype(jnp.bfloat16)

    repeat(total // chunk, build)

    col_wide = jnp.ones((REP, total), jnp.float32)
    for iteration in range(ITERS):
        row_sums = lax.dot_general(
            col_wide.astype(jnp.bfloat16), kern[...], (((1,), (1,)), ((), ())),
            preferred_element_type=jnp.float32,
        )
        row_scale = img_mass / row_sums
        partial_cols = jnp.dot(
            row_scale.astype(jnp.bfloat16), kern[...], preferred_element_type=jnp.float32
        )
        for line in range(lines):
            parts[iteration, my_inner, line : line + 1, :] = partial_cols[:1, line * LANES : (line + 1) * LANES]
        first = 2 + 2 * iteration
        mine = parts.at[iteration, my_inner]
        send(first, inner, near, lambda to: mine, mine)

        if iteration == ITERS - 1:
            row_feat = (img_unit.astype(jnp.float32) * row_scale[:1]).astype(jnp.bfloat16)
            for pair in range(n // 2):
                both = jnp.dot(
                    row_feat, kern[:, pair * LANES : (pair + 1) * LANES],
                    preferred_element_type=jnp.float32,
                )
                top, bottom = both[: FEAT // 2], both[FEAT // 2 :]
                feat_out[2 * pair] = jnp.where(left, top, pltpu.roll(bottom, HALF, 1)).astype(jnp.bfloat16)
                feat_out[2 * pair + 1] = jnp.where(left, pltpu.roll(top, HALF, 1), bottom).astype(jnp.bfloat16)
            send(1, n, partner, lambda to: feat_out.at[to], feat_in.at[me])

        arrived(first, inner, parts.at[iteration])
        sums[iteration, my_outer] = jnp.sum(parts[iteration], axis=0)
        group = sums.at[iteration, my_outer]
        send(first + 1, outer, far, lambda to: group, group)
        arrived(first + 1, outer, sums.at[iteration])
        col_sum = jnp.sum(sums[iteration], axis=0)
        scale[...] = mdl_mass_ref[...] / col_sum
        col_wide = jnp.concatenate(
            [jnp.broadcast_to(scale[line : line + 1, :], (REP, LANES)) for line in range(lines)], axis=1
        )

    weighted = (model[...].astype(jnp.float32) * col_wide[:1]).astype(jnp.bfloat16)
    image_terms = lax.dot_general(
        weighted, kern[...], (((1,), (1,)), ((), ())), preferred_element_type=jnp.float32
    )
    grad_img_ref[...] = -(image_terms * row_scale[:1])

    feat_in[me] = feat_out[me]
    arrived(1, n, feat_in)
    summed = jnp.sum(feat_in[...].astype(jnp.float32), axis=0)
    line = scale[pl.ds(me // 2, 1), :]
    even = lax.rem(me, 2) == 0
    own_scale = jnp.where(left[:1] == even, line, pltpu.roll(line, HALF, 1))
    packed = -(summed * own_scale)
    grad_mdl_ref[: FEAT // 2] = packed[:, :HALF]
    grad_mdl_ref[FEAT // 2 :] = pltpu.roll(packed, HALF, 1)[:, :HALF]

    sent(0, n, units)
    sent(1, n, feat_out)
    for iteration in range(ITERS):
        sent(2 + 2 * iteration, inner, parts.at[iteration])
        sent(3 + 2 * iteration, outer, sums.at[iteration])


def store_kernel(grad_img_ref, grad_mdl_ref, grad_img_hbm, grad_mdl_hbm, sems):
    stores = [
        pltpu.make_async_copy(grad_img_ref, grad_img_hbm, sems.at[0]),
        pltpu.make_async_copy(grad_mdl_ref, grad_mdl_hbm, sems.at[1]),
    ]
    for store in stores:
        store.start()
    for store in stores:
        store.wait()


def shards(n, img_feat, mdl_feat, img_mass, mdl_mass):
    rows = img_feat.shape[1]
    share = mdl_feat.shape[1]
    total = share * n
    assert share == HALF and img_feat.shape[0] == FEAT
    lines = total // LANES
    vmem = pl.BlockSpec(memory_space=pltpu.VMEM)
    packed = (n, FEAT // 2, LANES)
    anywhere = pl.BlockSpec(memory_space=pl.ANY)
    grads = pl.pallas_call(
        functools.partial(whole_kernel, n),
        out_shape=(
            pltpu.VMEM((FEAT, rows), jnp.float32),
            pltpu.VMEM((FEAT, share), jnp.float32),
        ),
        in_specs=[pl.BlockSpec(memory_space=pltpu.HBM)] * 4,
        out_specs=(vmem, vmem),
        scratch_shapes=[
            pltpu.VMEM((FEAT, rows), jnp.bfloat16),
            pltpu.VMEM((FEAT, share), jnp.bfloat16),
            pltpu.VMEM((1, rows), jnp.float32),
            pltpu.VMEM((lines, LANES), jnp.float32),
            pltpu.VMEM(packed, jnp.bfloat16),
            pltpu.VMEM((FEAT, total), jnp.bfloat16),
            pltpu.VMEM((rows, total), jnp.bfloat16),
            pltpu.VMEM((ITERS, near_group(n), lines, LANES), jnp.float32),
            pltpu.VMEM((ITERS, n // near_group(n), lines, LANES), jnp.float32),
            pltpu.VMEM((lines, LANES), jnp.float32),
            pltpu.VMEM(packed, jnp.bfloat16),
            pltpu.VMEM(packed, jnp.bfloat16),
            pltpu.SemaphoreType.DMA((4,)),
            pltpu.SemaphoreType.DMA((2 + 2 * ITERS,)),
            pltpu.SemaphoreType.DMA((2 + 2 * ITERS,)),
        ],
        compiler_params=pltpu.CompilerParams(
            collective_id=0, has_side_effects=True, vmem_limit_bytes=60 * 2**20
        ),
        name="sinkhorn",
    )(img_feat, mdl_feat, img_mass.reshape(1, rows), mdl_mass.reshape(lines, LANES))
    return pl.pallas_call(
        store_kernel,
        out_shape=(
            jax.ShapeDtypeStruct((FEAT, rows), jnp.float32),
            jax.ShapeDtypeStruct((FEAT, share), jnp.float32),
        ),
        in_specs=[vmem] * 2,
        out_specs=(anywhere, anywhere),
        scratch_shapes=[pltpu.SemaphoreType.DMA((2,))],
        compiler_params=pltpu.CompilerParams(vmem_limit_bytes=2**20),
        name="store",
    )(*grads)


def solution(mesh):
    placed = (P(None, ("fish", "img")), P(None, ("fish", "img")), P(("fish", "img")), P("fish"))
    return jax.shard_map(
        functools.partial(shards, mesh.shape["img"]),
        mesh=mesh,
        in_specs=placed,
        out_specs=(P(None, ("fish", "img")), P(None, ("fish", "img"))),
        check_vma=False,
    )
```

```python
import functools

import jax
import jax.numpy as jnp
from jax import lax
from jax.experimental import pallas as pl
from jax.experimental.pallas import tpu as pltpu
from jax.sharding import PartitionSpec as P

FEAT = 64
ITERS = 4
LANES = 128
HALF = 64
REP = 16

inv_temp = 20.0


def normalize(features):
    wide = features.astype(jnp.float32)
    guarded = jnp.mean(wide * wide, axis=0, keepdims=True) + 1e-06
    return wide * lax.rsqrt(guarded)


def repeat(count, body, carry=0):
    if count <= 16:
        for step in range(count):
            carry = body(step, carry)
        return carry
    return lax.fori_loop(0, count, body, carry)


def other(index, step, count):
    if not isinstance(step, int) or count & (count - 1):
        return lax.rem(index + step, count)
    bit = 1
    while bit <= step:
        if step & bit:
            index = index + bit * (1 - 2 * lax.rem(index // bit, 2))
        bit *= 2
    return index


def whole_kernel(
    n, img_hbm, mdl_hbm, img_mass_hbm, mdl_mass_hbm, grad_img_ref, grad_mdl_ref,
    img_ref, mdl_ref, img_mass_ref, mdl_mass_ref,
    units, model, kern, parts, scale, feat_out, feat_in, load_sem, unit_sem, send_sem, recv_sem,
):
    me = lax.axis_index("img")
    total = kern.shape[1]
    lines = total // LANES

    def partner(step):
        return other(me, n - 1 - step, n)

    def send(phase, source, target_slot, landed):
        def one(step, carry):
            to = partner(step)
            pltpu.make_async_remote_copy(
                src_ref=source(to),
                dst_ref=target_slot,
                send_sem=send_sem.at[phase],
                recv_sem=landed,
                device_id={"img": to},
                device_id_type=pl.DeviceIdType.MESH,
            ).start()
            return carry

        repeat(n - 1, one)

    def arrived(phase, slots):
        all_but_own = slots.at[pl.ds(0, n - 1)]
        pltpu.make_async_copy(all_but_own, all_but_own, recv_sem.at[phase]).wait()

    def sent(phase, slots):
        all_but_own = slots.at[pl.ds(0, n - 1)]
        pltpu.make_async_copy(all_but_own, all_but_own, send_sem.at[phase]).wait()

    barrier = pltpu.get_barrier_semaphore()

    def greet(step, carry):
        pl.semaphore_signal(
            barrier, inc=1, device_id={"img": partner(step)}, device_id_type=pl.DeviceIdType.MESH
        )
        return carry

    loads = [
        pltpu.make_async_copy(source, target, load_sem.at[slot])
        for slot, (source, target) in enumerate(
            ((mdl_hbm, mdl_ref), (img_hbm, img_ref), (img_mass_hbm, img_mass_ref), (mdl_mass_hbm, mdl_mass_ref))
        )
    ]
    for load in loads:
        load.start()
    repeat(n - 1, greet)
    loads[0].wait()

    own = normalize(mdl_ref[...])
    units[me] = jnp.concatenate([own[: FEAT // 2], own[FEAT // 2 :]], axis=1).astype(jnp.bfloat16)
    pl.semaphore_wait(barrier, n - 1)
    send(0, lambda to: units.at[me], units.at[me], unit_sem.at[me])

    for load in loads[1:]:
        load.wait()
    img_unit = normalize(img_ref[...]).astype(jnp.bfloat16)
    img_rows = img_unit.astype(jnp.float32).T.astype(jnp.bfloat16)
    img_mass = img_mass_ref[...]
    left = lax.broadcasted_iota(jnp.int32, (FEAT // 2, LANES), 1) < HALF

    factor = inv_temp / FEAT
    chunk = 2 * LANES
    group = chunk // HALF
    ones = jnp.ones((REP, chunk), jnp.bfloat16)

    def build(step, row_sums):
        which = other(me // group, step, n // group)
        for sub in range(group):
            sender = which * group + sub

            @pl.when(sender != me)
            def _():
                pltpu.make_async_copy(units.at[sender], units.at[sender], unit_sem.at[sender]).wait()

        blocks = []
        for sub in range(0, group, 2):
            one = units[which * group + sub].astype(jnp.float32)
            two = units[which * group + sub + 1].astype(jnp.float32)
            top = jnp.where(left, one, pltpu.roll(two, HALF, 1))
            bottom = jnp.where(left, pltpu.roll(one, HALF, 1), two)
            blocks.append(jnp.concatenate([top, bottom], axis=0))
        columns = jnp.concatenate(blocks, axis=1).astype(jnp.bfloat16)
        where = pl.ds(pl.multiple_of(which * chunk, chunk), chunk)
        model[:, where] = columns
        scores = jnp.dot(img_rows, columns, preferred_element_type=jnp.float32)
        tile = jnp.exp(scores * factor).astype(jnp.bfloat16)
        kern[:, where] = tile
        return row_sums + lax.dot_general(
            ones, tile, (((1,), (1,)), ((), ())), preferred_element_type=jnp.float32
        )

    row_sums = repeat(total // chunk, build, jnp.zeros((REP, kern.shape[0]), jnp.float32))

    for iteration in range(ITERS):
        if iteration > 0:
            row_sums = lax.dot_general(
                col_wide.astype(jnp.bfloat16), kern[...], (((1,), (1,)), ((), ())),
                preferred_element_type=jnp.float32,
            )
        row_scale = img_mass / row_sums
        partial_cols = jnp.dot(
            row_scale.astype(jnp.bfloat16), kern[...], preferred_element_type=jnp.float32
        )
        for line in range(lines):
            parts[iteration, me, line : line + 1, :] = partial_cols[:1, line * LANES : (line + 1) * LANES]
        send(1 + iteration, lambda to: parts.at[iteration, me], parts.at[iteration, me], recv_sem.at[1 + iteration])

        if iteration == ITERS - 1:
            row_feat = (img_unit.astype(jnp.float32) * row_scale[:1]).astype(jnp.bfloat16)
            for pair in range(n // 2):
                both = jnp.dot(
                    row_feat, kern[:, pair * LANES : (pair + 1) * LANES],
                    preferred_element_type=jnp.float32,
                )
                top, bottom = both[: FEAT // 2], both[FEAT // 2 :]
                feat_out[2 * pair] = jnp.where(left, top, pltpu.roll(bottom, HALF, 1)).astype(jnp.bfloat16)
                feat_out[2 * pair + 1] = jnp.where(left, pltpu.roll(top, HALF, 1), bottom).astype(jnp.bfloat16)
            send(1 + ITERS, lambda to: feat_out.at[to], feat_in.at[me], recv_sem.at[1 + ITERS])

        arrived(1 + iteration, parts.at[iteration])
        col_sum = jnp.sum(parts[iteration], axis=0)
        scale[...] = mdl_mass_ref[...] / col_sum
        col_wide = jnp.concatenate(
            [jnp.broadcast_to(scale[line : line + 1, :], (REP, LANES)) for line in range(lines)], axis=1
        )

    weighted = (model[...].astype(jnp.float32) * col_wide[:1]).astype(jnp.bfloat16)
    image_terms = lax.dot_general(
        weighted, kern[...], (((1,), (1,)), ((), ())), preferred_element_type=jnp.float32
    )
    grad_img_ref[...] = -(image_terms * row_scale[:1])

    feat_in[me] = feat_out[me]
    arrived(1 + ITERS, feat_in)
    summed = jnp.sum(feat_in[...].astype(jnp.float32), axis=0)
    line = scale[pl.ds(me // 2, 1), :]
    even = lax.rem(me, 2) == 0
    own_scale = jnp.where(left[:1] == even, line, pltpu.roll(line, HALF, 1))
    packed = -(summed * own_scale)
    grad_mdl_ref[: FEAT // 2] = packed[:, :HALF]
    grad_mdl_ref[FEAT // 2 :] = pltpu.roll(packed, HALF, 1)[:, :HALF]

    sent(0, units)
    for iteration in range(ITERS):
        sent(1 + iteration, parts.at[iteration])
    sent(1 + ITERS, feat_out)


def store_kernel(grad_img_ref, grad_mdl_ref, grad_img_hbm, grad_mdl_hbm, sems):
    stores = [
        pltpu.make_async_copy(grad_img_ref, grad_img_hbm, sems.at[0]),
        pltpu.make_async_copy(grad_mdl_ref, grad_mdl_hbm, sems.at[1]),
    ]
    for store in stores:
        store.start()
    for store in stores:
        store.wait()


def shards(n, img_feat, mdl_feat, img_mass, mdl_mass):
    rows = img_feat.shape[1]
    share = mdl_feat.shape[1]
    total = share * n
    assert share == HALF and img_feat.shape[0] == FEAT
    lines = total // LANES
    vmem = pl.BlockSpec(memory_space=pltpu.VMEM)
    packed = (n, FEAT // 2, LANES)
    anywhere = pl.BlockSpec(memory_space=pl.ANY)
    grads = pl.pallas_call(
        functools.partial(whole_kernel, n),
        out_shape=(
            pltpu.VMEM((FEAT, rows), jnp.float32),
            pltpu.VMEM((FEAT, share), jnp.float32),
        ),
        in_specs=[pl.BlockSpec(memory_space=pltpu.HBM)] * 4,
        out_specs=(vmem, vmem),
        scratch_shapes=[
            pltpu.VMEM((FEAT, rows), jnp.bfloat16),
            pltpu.VMEM((FEAT, share), jnp.bfloat16),
            pltpu.VMEM((1, rows), jnp.float32),
            pltpu.VMEM((lines, LANES), jnp.float32),
            pltpu.VMEM(packed, jnp.bfloat16),
            pltpu.VMEM((FEAT, total), jnp.bfloat16),
            pltpu.VMEM((rows, total), jnp.bfloat16),
            pltpu.VMEM((ITERS, n, lines, LANES), jnp.float32),
            pltpu.VMEM((lines, LANES), jnp.float32),
            pltpu.VMEM(packed, jnp.bfloat16),
            pltpu.VMEM(packed, jnp.bfloat16),
            pltpu.SemaphoreType.DMA((4,)),
            pltpu.SemaphoreType.DMA((n,)),
            pltpu.SemaphoreType.DMA((2 + ITERS,)),
            pltpu.SemaphoreType.DMA((2 + ITERS,)),
        ],
        compiler_params=pltpu.CompilerParams(
            collective_id=0, has_side_effects=True, vmem_limit_bytes=60 * 2**20
        ),
        name="sinkhorn",
    )(img_feat, mdl_feat, img_mass.reshape(1, rows), mdl_mass.reshape(lines, LANES))
    return pl.pallas_call(
        store_kernel,
        out_shape=(
            jax.ShapeDtypeStruct((FEAT, rows), jnp.float32),
            jax.ShapeDtypeStruct((FEAT, share), jnp.float32),
        ),
        in_specs=[vmem] * 2,
        out_specs=(anywhere, anywhere),
        scratch_shapes=[pltpu.SemaphoreType.DMA((2,))],
        compiler_params=pltpu.CompilerParams(vmem_limit_bytes=2**20),
        name="store",
    )(*grads)


def solution(mesh):
    placed = (P(None, ("fish", "img")), P(None, ("fish", "img")), P(("fish", "img")), P("fish"))
    return jax.shard_map(
        functools.partial(shards, mesh.shape["img"]),
        mesh=mesh,
        in_specs=placed,
        out_specs=(P(None, ("fish", "img")), P(None, ("fish", "img"))),
        check_vma=False,
    )
```

```python
import functools

import jax
import jax.numpy as jnp
from jax import lax
from jax.experimental import pallas as pl
from jax.experimental.pallas import tpu as pltpu
from jax.sharding import PartitionSpec as P

FEAT = 64
ITERS = 4
LANES = 128
HALF = 64

inv_temp = 20.0


def normalize(features):
    wide = features.astype(jnp.float32)
    guarded = jnp.mean(wide * wide, axis=0, keepdims=True) + 1e-06
    return wide * lax.rsqrt(guarded)


def repeat(count, body, carry=0):
    if count <= 16:
        for step in range(count):
            carry = body(step, carry)
        return carry
    return lax.fori_loop(0, count, body, carry)


def other(index, step, count):
    if not isinstance(step, int) or count & (count - 1):
        return lax.rem(index + step, count)
    bit = 1
    while bit <= step:
        if step & bit:
            index = index + bit * (1 - 2 * lax.rem(index // bit, 2))
        bit *= 2
    return index


def whole_kernel(
    n, img_hbm, mdl_hbm, img_mass_hbm, mdl_mass_hbm, grad_img_ref, grad_mdl_ref,
    img_ref, mdl_ref, img_mass_ref, mdl_mass_ref,
    units, model, kern, wide, row_scale, parts, scale, feat_out, feat_in, load_sem, unit_sem, send_sem, recv_sem,
):
    me = lax.axis_index("img")
    total = kern.shape[1]
    lines = total // LANES

    def partner(step):
        return other(me, n - 1 - step, n)

    def send(phase, source, target_slot, landed):
        def one(step, carry):
            to = partner(step)
            pltpu.make_async_remote_copy(
                src_ref=source(to),
                dst_ref=target_slot,
                send_sem=send_sem.at[phase],
                recv_sem=landed,
                device_id={"img": to},
                device_id_type=pl.DeviceIdType.MESH,
            ).start()
            return carry

        repeat(n - 1, one)

    def arrived(phase, slots):
        all_but_own = slots.at[pl.ds(0, n - 1)]
        pltpu.make_async_copy(all_but_own, all_but_own, recv_sem.at[phase]).wait()

    def sent(phase, slots):
        all_but_own = slots.at[pl.ds(0, n - 1)]
        pltpu.make_async_copy(all_but_own, all_but_own, send_sem.at[phase]).wait()

    barrier = pltpu.get_barrier_semaphore()

    def greet(step, carry):
        pl.semaphore_signal(
            barrier, inc=1, device_id={"img": partner(step)}, device_id_type=pl.DeviceIdType.MESH
        )
        return carry

    loads = [
        pltpu.make_async_copy(source, target, load_sem.at[slot])
        for slot, (source, target) in enumerate(
            ((mdl_hbm, mdl_ref), (img_hbm, img_ref), (img_mass_hbm, img_mass_ref), (mdl_mass_hbm, mdl_mass_ref))
        )
    ]
    for load in loads:
        load.start()
    repeat(n - 1, greet)
    loads[0].wait()

    own = normalize(mdl_ref[...])
    units[me] = jnp.concatenate([own[: FEAT // 2], own[FEAT // 2 :]], axis=1).astype(jnp.bfloat16)
    pl.semaphore_wait(barrier, n - 1)
    send(0, lambda to: units.at[me], units.at[me], unit_sem.at[me])

    for load in loads[1:]:
        load.wait()
    img_unit = normalize(img_ref[...]).astype(jnp.bfloat16)
    img_rows = img_unit.astype(jnp.float32).T.astype(jnp.bfloat16)
    img_mass = jnp.broadcast_to(img_mass_ref[...], (LANES, img_rows.shape[0])).T
    left = lax.broadcasted_iota(jnp.int32, (FEAT // 2, LANES), 1) < HALF

    factor = inv_temp / FEAT
    chunk = 2 * LANES
    group = chunk // HALF
    rows = kern.shape[0]
    block = 64

    def build(step, row_sums):
        which = other(me // group, step, n // group)
        for sub in range(group):
            sender = which * group + sub

            @pl.when(sender != me)
            def _():
                pltpu.make_async_copy(units.at[sender], units.at[sender], unit_sem.at[sender]).wait()

        blocks = []
        for sub in range(0, group, 2):
            one = units[which * group + sub].astype(jnp.float32)
            two = units[which * group + sub + 1].astype(jnp.float32)
            top = jnp.where(left, one, pltpu.roll(two, HALF, 1))
            bottom = jnp.where(left, pltpu.roll(one, HALF, 1), two)
            blocks.append(jnp.concatenate([top, bottom], axis=0))
        columns = jnp.concatenate(blocks, axis=1).astype(jnp.bfloat16)
        where = pl.ds(pl.multiple_of(which * chunk, chunk), chunk)
        model[:, where] = columns
        scores = jnp.dot(img_rows, columns, preferred_element_type=jnp.float32)
        tile = jnp.exp(scores * factor).astype(jnp.bfloat16)
        kern[:, where] = tile
        tile = tile.astype(jnp.float32)
        wide[:, where] = tile
        for line in range(chunk // LANES):
            row_sums += tile[:, line * LANES : (line + 1) * LANES]
        return row_sums

    row_sums = repeat(total // chunk, build, jnp.zeros((rows, LANES), jnp.float32))

    for iteration in range(ITERS):
        for start in range(0, rows, block):
            here = slice(start, start + block)
            if iteration == 0:
                by_lane = row_sums[here]
            else:
                by_lane = jnp.zeros((block, LANES), jnp.float32)
                for line in range(lines):
                    by_lane += wide[here, line * LANES : (line + 1) * LANES] * col_low[line : line + 1]
            row_scale[here] = img_mass[here] / jnp.sum(by_lane, axis=1, keepdims=True)
        partial_cols = jnp.zeros((8, total), jnp.float32)
        for start in range(0, rows, block):
            here = slice(start, start + block)
            row_low = row_scale[here, :1].astype(jnp.bfloat16).astype(jnp.float32)
            partial_cols += jnp.sum((wide[here] * row_low).reshape(block // 8, 8, total), axis=0)
        partial_cols = jnp.sum(partial_cols, axis=0, keepdims=True)
        for line in range(lines):
            parts[iteration, me, line : line + 1, :] = partial_cols[:, line * LANES : (line + 1) * LANES]
        send(1 + iteration, lambda to: parts.at[iteration, me], parts.at[iteration, me], recv_sem.at[1 + iteration])

        if iteration == ITERS - 1:
            row_line = row_scale[...].T[:1]
            row_feat = (img_unit.astype(jnp.float32) * row_line).astype(jnp.bfloat16)
            for pair in range(n // 2):
                both = jnp.dot(
                    row_feat, kern[:, pair * LANES : (pair + 1) * LANES],
                    preferred_element_type=jnp.float32,
                )
                top, bottom = both[: FEAT // 2], both[FEAT // 2 :]
                feat_out[2 * pair] = jnp.where(left, top, pltpu.roll(bottom, HALF, 1)).astype(jnp.bfloat16)
                feat_out[2 * pair + 1] = jnp.where(left, pltpu.roll(top, HALF, 1), bottom).astype(jnp.bfloat16)
            send(1 + ITERS, lambda to: feat_out.at[to], feat_in.at[me], recv_sem.at[1 + ITERS])

        arrived(1 + iteration, parts.at[iteration])
        col_sum = jnp.sum(parts[iteration], axis=0)
        scale[...] = mdl_mass_ref[...] / col_sum
        col_low = scale[...].astype(jnp.bfloat16).astype(jnp.float32)

    col_line = jnp.concatenate([scale[line : line + 1, :] for line in range(lines)], axis=1)
    weighted = (model[...].astype(jnp.float32) * col_line).astype(jnp.bfloat16)
    image_terms = lax.dot_general(
        weighted, kern[...], (((1,), (1,)), ((), ())), preferred_element_type=jnp.float32
    )
    grad_img_ref[...] = -(image_terms * row_line)

    feat_in[me] = feat_out[me]
    arrived(1 + ITERS, feat_in)
    summed = jnp.sum(feat_in[...].astype(jnp.float32), axis=0)
    line = scale[pl.ds(me // 2, 1), :]
    even = lax.rem(me, 2) == 0
    own_scale = jnp.where(left[:1] == even, line, pltpu.roll(line, HALF, 1))
    packed = -(summed * own_scale)
    grad_mdl_ref[: FEAT // 2] = packed[:, :HALF]
    grad_mdl_ref[FEAT // 2 :] = pltpu.roll(packed, HALF, 1)[:, :HALF]

    sent(0, units)
    for iteration in range(ITERS):
        sent(1 + iteration, parts.at[iteration])
    sent(1 + ITERS, feat_out)


def store_kernel(grad_img_ref, grad_mdl_ref, grad_img_hbm, grad_mdl_hbm, sems):
    stores = [
        pltpu.make_async_copy(grad_img_ref, grad_img_hbm, sems.at[0]),
        pltpu.make_async_copy(grad_mdl_ref, grad_mdl_hbm, sems.at[1]),
    ]
    for store in stores:
        store.start()
    for store in stores:
        store.wait()


def shards(n, img_feat, mdl_feat, img_mass, mdl_mass):
    rows = img_feat.shape[1]
    share = mdl_feat.shape[1]
    total = share * n
    assert share == HALF and img_feat.shape[0] == FEAT
    lines = total // LANES
    vmem = pl.BlockSpec(memory_space=pltpu.VMEM)
    packed = (n, FEAT // 2, LANES)
    anywhere = pl.BlockSpec(memory_space=pl.ANY)
    grads = pl.pallas_call(
        functools.partial(whole_kernel, n),
        out_shape=(
            pltpu.VMEM((FEAT, rows), jnp.float32),
            pltpu.VMEM((FEAT, share), jnp.float32),
        ),
        in_specs=[pl.BlockSpec(memory_space=pltpu.HBM)] * 4,
        out_specs=(vmem, vmem),
        scratch_shapes=[
            pltpu.VMEM((FEAT, rows), jnp.bfloat16),
            pltpu.VMEM((FEAT, share), jnp.bfloat16),
            pltpu.VMEM((1, rows), jnp.float32),
            pltpu.VMEM((lines, LANES), jnp.float32),
            pltpu.VMEM(packed, jnp.bfloat16),
            pltpu.VMEM((FEAT, total), jnp.bfloat16),
            pltpu.VMEM((rows, total), jnp.bfloat16),
            pltpu.VMEM((rows, total), jnp.float32),
            pltpu.VMEM((rows, LANES), jnp.float32),
            pltpu.VMEM((ITERS, n, lines, LANES), jnp.float32),
            pltpu.VMEM((lines, LANES), jnp.float32),
            pltpu.VMEM(packed, jnp.bfloat16),
            pltpu.VMEM(packed, jnp.bfloat16),
            pltpu.SemaphoreType.DMA((4,)),
            pltpu.SemaphoreType.DMA((n,)),
            pltpu.SemaphoreType.DMA((2 + ITERS,)),
            pltpu.SemaphoreType.DMA((2 + ITERS,)),
        ],
        compiler_params=pltpu.CompilerParams(
            collective_id=0, has_side_effects=True, vmem_limit_bytes=60 * 2**20
        ),
        name="sinkhorn",
    )(img_feat, mdl_feat, img_mass.reshape(1, rows), mdl_mass.reshape(lines, LANES))
    return pl.pallas_call(
        store_kernel,
        out_shape=(
            jax.ShapeDtypeStruct((FEAT, rows), jnp.float32),
            jax.ShapeDtypeStruct((FEAT, share), jnp.float32),
        ),
        in_specs=[vmem] * 2,
        out_specs=(anywhere, anywhere),
        scratch_shapes=[pltpu.SemaphoreType.DMA((2,))],
        compiler_params=pltpu.CompilerParams(vmem_limit_bytes=2**20),
        name="store",
    )(*grads)


def solution(mesh):
    placed = (P(None, ("fish", "img")), P(None, ("fish", "img")), P(("fish", "img")), P("fish"))
    return jax.shard_map(
        functools.partial(shards, mesh.shape["img"]),
        mesh=mesh,
        in_specs=placed,
        out_specs=(P(None, ("fish", "img")), P(None, ("fish", "img"))),
        check_vma=False,
    )
```

```python
import functools

import jax
import jax.numpy as jnp
from jax import lax
from jax.experimental import pallas as pl
from jax.experimental.pallas import tpu as pltpu
from jax.sharding import PartitionSpec as P

FEAT = 64
ITERS = 4
LANES = 128
HALF = 64

inv_temp = 20.0


def normalize(features):
    wide = features.astype(jnp.float32)
    guarded = jnp.mean(wide * wide, axis=0, keepdims=True) + 1e-06
    return wide * lax.rsqrt(guarded)


def repeat(count, body, carry=0):
    if count <= 16:
        for step in range(count):
            carry = body(step, carry)
        return carry
    return lax.fori_loop(0, count, body, carry)


def other(index, step, count):
    if not isinstance(step, int) or count & (count - 1):
        return lax.rem(index + step, count)
    bit = 1
    while bit <= step:
        if step & bit:
            index = index + bit * (1 - 2 * lax.rem(index // bit, 2))
        bit *= 2
    return index


def whole_kernel(
    n, img_hbm, mdl_hbm, img_mass_hbm, mdl_mass_hbm, grad_img_ref, grad_mdl_ref,
    img_ref, mdl_ref, img_mass_ref, mdl_mass_ref,
    units, model, kern, wide, row_scale, parts, scale, feat_out, feat_in, load_sem, unit_sem, send_sem, recv_sem,
):
    me = lax.axis_index("img")
    total = kern.shape[1]
    lines = total // LANES

    def partner(step):
        return other(me, n - 1 - step, n)

    def send(phase, source, target_slot, landed):
        def one(step, carry):
            to = partner(step)
            pltpu.make_async_remote_copy(
                src_ref=source(to),
                dst_ref=target_slot,
                send_sem=send_sem.at[phase],
                recv_sem=landed,
                device_id={"img": to},
                device_id_type=pl.DeviceIdType.MESH,
            ).start()
            return carry

        repeat(n - 1, one)

    def arrived(phase, slots):
        all_but_own = slots.at[pl.ds(0, n - 1)]
        pltpu.make_async_copy(all_but_own, all_but_own, recv_sem.at[phase]).wait()

    def sent(phase, slots):
        all_but_own = slots.at[pl.ds(0, n - 1)]
        pltpu.make_async_copy(all_but_own, all_but_own, send_sem.at[phase]).wait()

    barrier = pltpu.get_barrier_semaphore()

    def greet(step, carry):
        pl.semaphore_signal(
            barrier, inc=1, device_id={"img": partner(step)}, device_id_type=pl.DeviceIdType.MESH
        )
        return carry

    loads = [
        pltpu.make_async_copy(source, target, load_sem.at[slot])
        for slot, (source, target) in enumerate(
            ((mdl_hbm, mdl_ref), (img_hbm, img_ref), (img_mass_hbm, img_mass_ref), (mdl_mass_hbm, mdl_mass_ref))
        )
    ]
    for load in loads:
        load.start()
    repeat(n - 1, greet)
    loads[0].wait()

    own = normalize(mdl_ref[...])
    units[me] = jnp.concatenate([own[: FEAT // 2], own[FEAT // 2 :]], axis=1).astype(jnp.bfloat16)
    pl.semaphore_wait(barrier, n - 1)
    send(0, lambda to: units.at[me], units.at[me], unit_sem.at[me])

    for load in loads[1:]:
        load.wait()
    img_unit = normalize(img_ref[...]).astype(jnp.bfloat16)
    img_rows = img_unit.astype(jnp.float32).T.astype(jnp.bfloat16)
    img_mass = jnp.broadcast_to(img_mass_ref[...], (LANES, img_rows.shape[0])).T
    left = lax.broadcasted_iota(jnp.int32, (FEAT // 2, LANES), 1) < HALF

    factor = inv_temp / FEAT
    chunk = 2 * LANES
    group = chunk // HALF
    rows = kern.shape[0]
    block = 64

    def build(step, row_sums):
        which = other(me // group, step, n // group)
        for sub in range(group):
            sender = which * group + sub

            @pl.when(sender != me)
            def _():
                pltpu.make_async_copy(units.at[sender], units.at[sender], unit_sem.at[sender]).wait()

        blocks = []
        for sub in range(0, group, 2):
            one = units[which * group + sub].astype(jnp.float32)
            two = units[which * group + sub + 1].astype(jnp.float32)
            top = jnp.where(left, one, pltpu.roll(two, HALF, 1))
            bottom = jnp.where(left, pltpu.roll(one, HALF, 1), two)
            blocks.append(jnp.concatenate([top, bottom], axis=0))
        columns = jnp.concatenate(blocks, axis=1).astype(jnp.bfloat16)
        where = pl.ds(pl.multiple_of(which * chunk, chunk), chunk)
        model[:, where] = columns
        scores = jnp.dot(img_rows, columns, preferred_element_type=jnp.float32)
        tile = jnp.exp(scores * factor).astype(jnp.bfloat16)
        kern[:, where] = tile
        tile = tile.astype(jnp.float32)
        wide[:, where] = tile
        for line in range(chunk // LANES):
            row_sums += tile[:, line * LANES : (line + 1) * LANES]
        return row_sums

    row_sums = repeat(total // chunk, build, jnp.zeros((rows, LANES), jnp.float32))

    for iteration in range(ITERS):
        for start in range(0, rows, block):
            here = slice(start, start + block)
            if iteration == 0:
                by_lane = row_sums[here]
            else:
                by_lane = jnp.zeros((block, LANES), jnp.float32)
                for line in range(lines):
                    by_lane += wide[here, line * LANES : (line + 1) * LANES] * col_low[line : line + 1]
            row_scale[here] = img_mass[here] / jnp.sum(by_lane, axis=1, keepdims=True)
        partial_cols = jnp.zeros((8, total), jnp.float32)
        for start in range(0, rows, block):
            here = slice(start, start + block)
            row_low = row_scale[here, :1].astype(jnp.bfloat16).astype(jnp.float32)
            partial_cols += jnp.sum((wide[here] * row_low).reshape(block // 8, 8, total), axis=0)
        partial_cols = jnp.sum(partial_cols, axis=0, keepdims=True)
        for line in range(lines):
            scale[line : line + 1, :] = partial_cols[:, line * LANES : (line + 1) * LANES]
        parts[iteration, me] = scale[...].astype(jnp.bfloat16)
        send(1 + iteration, lambda to: parts.at[iteration, me], parts.at[iteration, me], recv_sem.at[1 + iteration])

        if iteration == ITERS - 1:
            row_line = row_scale[...].T[:1]
            row_feat = (img_unit.astype(jnp.float32) * row_line).astype(jnp.bfloat16)
            for pair in range(n // 2):
                both = jnp.dot(
                    row_feat, kern[:, pair * LANES : (pair + 1) * LANES],
                    preferred_element_type=jnp.float32,
                )
                top, bottom = both[: FEAT // 2], both[FEAT // 2 :]
                feat_out[2 * pair] = jnp.where(left, top, pltpu.roll(bottom, HALF, 1)).astype(jnp.bfloat16)
                feat_out[2 * pair + 1] = jnp.where(left, pltpu.roll(top, HALF, 1), bottom).astype(jnp.bfloat16)
            send(1 + ITERS, lambda to: feat_out.at[to], feat_in.at[me], recv_sem.at[1 + ITERS])

        arrived(1 + iteration, parts.at[iteration])
        col_sum = jnp.sum(parts[iteration].astype(jnp.float32), axis=0)
        scale[...] = mdl_mass_ref[...] / col_sum
        col_low = scale[...].astype(jnp.bfloat16).astype(jnp.float32)

    col_line = jnp.concatenate([scale[line : line + 1, :] for line in range(lines)], axis=1)
    weighted = (model[...].astype(jnp.float32) * col_line).astype(jnp.bfloat16)
    image_terms = lax.dot_general(
        weighted, kern[...], (((1,), (1,)), ((), ())), preferred_element_type=jnp.float32
    )
    grad_img_ref[...] = -(image_terms * row_line)

    feat_in[me] = feat_out[me]
    arrived(1 + ITERS, feat_in)
    summed = jnp.sum(feat_in[...].astype(jnp.float32), axis=0)
    line = scale[pl.ds(me // 2, 1), :]
    even = lax.rem(me, 2) == 0
    own_scale = jnp.where(left[:1] == even, line, pltpu.roll(line, HALF, 1))
    packed = -(summed * own_scale)
    grad_mdl_ref[: FEAT // 2] = packed[:, :HALF]
    grad_mdl_ref[FEAT // 2 :] = pltpu.roll(packed, HALF, 1)[:, :HALF]

    sent(0, units)
    for iteration in range(ITERS):
        sent(1 + iteration, parts.at[iteration])
    sent(1 + ITERS, feat_out)


def store_kernel(grad_img_ref, grad_mdl_ref, grad_img_hbm, grad_mdl_hbm, sems):
    stores = [
        pltpu.make_async_copy(grad_img_ref, grad_img_hbm, sems.at[0]),
        pltpu.make_async_copy(grad_mdl_ref, grad_mdl_hbm, sems.at[1]),
    ]
    for store in stores:
        store.start()
    for store in stores:
        store.wait()


def shards(n, img_feat, mdl_feat, img_mass, mdl_mass):
    rows = img_feat.shape[1]
    share = mdl_feat.shape[1]
    total = share * n
    assert share == HALF and img_feat.shape[0] == FEAT
    lines = total // LANES
    vmem = pl.BlockSpec(memory_space=pltpu.VMEM)
    packed = (n, FEAT // 2, LANES)
    anywhere = pl.BlockSpec(memory_space=pl.ANY)
    grads = pl.pallas_call(
        functools.partial(whole_kernel, n),
        out_shape=(
            pltpu.VMEM((FEAT, rows), jnp.float32),
            pltpu.VMEM((FEAT, share), jnp.float32),
        ),
        in_specs=[pl.BlockSpec(memory_space=pltpu.HBM)] * 4,
        out_specs=(vmem, vmem),
        scratch_shapes=[
            pltpu.VMEM((FEAT, rows), jnp.bfloat16),
            pltpu.VMEM((FEAT, share), jnp.bfloat16),
            pltpu.VMEM((1, rows), jnp.float32),
            pltpu.VMEM((lines, LANES), jnp.float32),
            pltpu.VMEM(packed, jnp.bfloat16),
            pltpu.VMEM((FEAT, total), jnp.bfloat16),
            pltpu.VMEM((rows, total), jnp.bfloat16),
            pltpu.VMEM((rows, total), jnp.float32),
            pltpu.VMEM((rows, LANES), jnp.float32),
            pltpu.VMEM((ITERS, n, lines, LANES), jnp.bfloat16),
            pltpu.VMEM((lines, LANES), jnp.float32),
            pltpu.VMEM(packed, jnp.bfloat16),
            pltpu.VMEM(packed, jnp.bfloat16),
            pltpu.SemaphoreType.DMA((4,)),
            pltpu.SemaphoreType.DMA((n,)),
            pltpu.SemaphoreType.DMA((2 + ITERS,)),
            pltpu.SemaphoreType.DMA((2 + ITERS,)),
        ],
        compiler_params=pltpu.CompilerParams(
            collective_id=0, has_side_effects=True, vmem_limit_bytes=60 * 2**20
        ),
        name="sinkhorn",
    )(img_feat, mdl_feat, img_mass.reshape(1, rows), mdl_mass.reshape(lines, LANES))
    return pl.pallas_call(
        store_kernel,
        out_shape=(
            jax.ShapeDtypeStruct((FEAT, rows), jnp.float32),
            jax.ShapeDtypeStruct((FEAT, share), jnp.float32),
        ),
        in_specs=[vmem] * 2,
        out_specs=(anywhere, anywhere),
        scratch_shapes=[pltpu.SemaphoreType.DMA((2,))],
        compiler_params=pltpu.CompilerParams(vmem_limit_bytes=2**20),
        name="store",
    )(*grads)


def solution(mesh):
    placed = (P(None, ("fish", "img")), P(None, ("fish", "img")), P(("fish", "img")), P("fish"))
    return jax.shard_map(
        functools.partial(shards, mesh.shape["img"]),
        mesh=mesh,
        in_specs=placed,
        out_specs=(P(None, ("fish", "img")), P(None, ("fish", "img"))),
        check_vma=False,
    )
```

```python
import functools

import jax
import jax.numpy as jnp
from jax import lax
from jax.experimental import pallas as pl
from jax.experimental.pallas import tpu as pltpu
from jax.sharding import PartitionSpec as P

FEAT = 64
ITERS = 4
LANES = 128
HALF = 64

inv_temp = 20.0


def normalize(features):
    wide = features.astype(jnp.float32)
    guarded = jnp.mean(wide * wide, axis=0, keepdims=True) + 1e-06
    return wide * lax.rsqrt(guarded)


def repeat(count, body, carry=0):
    if count <= 16:
        for step in range(count):
            carry = body(step, carry)
        return carry
    return lax.fori_loop(0, count, body, carry)


def other(index, step, count):
    if not isinstance(step, int) or count & (count - 1):
        return lax.rem(index + step, count)
    bit = 1
    while bit <= step:
        if step & bit:
            index = index + bit * (1 - 2 * lax.rem(index // bit, 2))
        bit *= 2
    return index


def whole_kernel(
    n, img_hbm, mdl_hbm, img_mass_hbm, mdl_mass_hbm, grad_img_ref, grad_mdl_ref,
    img_ref, mdl_ref, img_mass_ref, mdl_mass_ref,
    units, model, kern, wide, row_scale, parts, scale, feat_out, feat_in, load_sem, unit_sem, send_sem, recv_sem,
):
    me = lax.axis_index("img")
    total = kern.shape[1]
    lines = total // LANES

    partners = [other(me, n - 1 - step, n) for step in range(n - 1)] if n <= 16 else None

    def partner(step):
        return partners[step] if partners else other(me, step + 1, n)

    def send(phase, source, target_slot, landed):
        def one(step, carry):
            to = partner(step)
            pltpu.make_async_remote_copy(
                src_ref=source(to),
                dst_ref=target_slot,
                send_sem=send_sem.at[phase],
                recv_sem=landed,
                device_id={"img": to},
                device_id_type=pl.DeviceIdType.MESH,
            ).start()
            return carry

        repeat(n - 1, one)

    def arrived(phase, slots):
        all_but_own = slots.at[pl.ds(0, n - 1)]
        pltpu.make_async_copy(all_but_own, all_but_own, recv_sem.at[phase]).wait()

    def sent(phase, slots):
        all_but_own = slots.at[pl.ds(0, n - 1)]
        pltpu.make_async_copy(all_but_own, all_but_own, send_sem.at[phase]).wait()

    barrier = pltpu.get_barrier_semaphore()

    def greet(step, carry):
        pl.semaphore_signal(
            barrier, inc=1, device_id={"img": partner(step)}, device_id_type=pl.DeviceIdType.MESH
        )
        return carry

    loads = [
        pltpu.make_async_copy(source, target, load_sem.at[slot])
        for slot, (source, target) in enumerate(
            ((mdl_hbm, mdl_ref), (img_hbm, img_ref), (img_mass_hbm, img_mass_ref), (mdl_mass_hbm, mdl_mass_ref))
        )
    ]
    for load in loads:
        load.start()
    repeat(n - 1, greet)
    loads[0].wait()

    own = normalize(mdl_ref[...])
    units[me] = jnp.concatenate([own[: FEAT // 2], own[FEAT // 2 :]], axis=1).astype(jnp.bfloat16)
    pl.semaphore_wait(barrier, n - 1)
    send(0, lambda to: units.at[me], units.at[me], unit_sem.at[me])

    for load in loads[1:]:
        load.wait()
    img_unit = normalize(img_ref[...]).astype(jnp.bfloat16)
    img_rows = img_unit.astype(jnp.float32).T.astype(jnp.bfloat16)
    img_mass = jnp.broadcast_to(img_mass_ref[...], (LANES, img_rows.shape[0])).T
    left = lax.broadcasted_iota(jnp.int32, (FEAT // 2, LANES), 1) < HALF

    factor = inv_temp / FEAT
    chunk = 2 * LANES
    group = chunk // HALF
    rows = kern.shape[0]
    block = 64

    def build(step, row_sums):
        which = other(me // group, step, n // group)
        for sub in range(group):
            sender = which * group + sub

            @pl.when(sender != me)
            def _():
                pltpu.make_async_copy(units.at[sender], units.at[sender], unit_sem.at[sender]).wait()

        blocks = []
        for sub in range(0, group, 2):
            one = units[which * group + sub].astype(jnp.float32)
            two = units[which * group + sub + 1].astype(jnp.float32)
            top = jnp.where(left, one, pltpu.roll(two, HALF, 1))
            bottom = jnp.where(left, pltpu.roll(one, HALF, 1), two)
            blocks.append(jnp.concatenate([top, bottom], axis=0))
        columns = jnp.concatenate(blocks, axis=1).astype(jnp.bfloat16)
        where = pl.ds(pl.multiple_of(which * chunk, chunk), chunk)
        model[:, where] = columns
        scores = jnp.dot(img_rows, columns, preferred_element_type=jnp.float32)
        tile = jnp.exp(scores * factor).astype(jnp.bfloat16)
        kern[:, where] = tile
        tile = tile.astype(jnp.float32)
        wide[:, where] = tile
        for line in range(chunk // LANES):
            row_sums += tile[:, line * LANES : (line + 1) * LANES]
        return row_sums

    row_sums = repeat(total // chunk, build, jnp.zeros((rows, LANES), jnp.float32))

    for iteration in range(ITERS):
        partial_cols = jnp.zeros((8, total), jnp.float32)
        for start in range(0, rows, block):
            here = slice(start, start + block)
            if iteration == 0:
                by_lane = row_sums[here]
            else:
                by_lane = wide[here, :LANES] * col_low[0]
                for line in range(1, lines):
                    by_lane += wide[here, line * LANES : (line + 1) * LANES] * col_low[line]
            scaled = img_mass[here] / jnp.broadcast_to(jnp.sum(by_lane, axis=1, keepdims=True), (block, LANES))
            if iteration == ITERS - 1:
                row_scale[here] = scaled
            row_low = scaled.astype(jnp.bfloat16).astype(jnp.float32)
            row_low = jnp.concatenate([row_low] * lines, axis=1)
            partial_cols += jnp.sum((wide[here] * row_low).reshape(block // 8, 8, total), axis=0)
        partial_cols = jnp.sum(partial_cols, axis=0, keepdims=True)
        for line in range(lines):
            scale[line : line + 1, :] = partial_cols[:, line * LANES : (line + 1) * LANES]
        parts[iteration, me] = scale[...].astype(jnp.bfloat16)
        send(1 + iteration, lambda to: parts.at[iteration, me], parts.at[iteration, me], recv_sem.at[1 + iteration])

        if iteration == ITERS - 1:
            row_line = row_scale[...].T[:1]
            row_feat = (img_unit.astype(jnp.float32) * row_line).astype(jnp.bfloat16)
            for quad in range(n // 4):
                four = jnp.dot(
                    row_feat, kern[:, quad * chunk : (quad + 1) * chunk],
                    preferred_element_type=jnp.float32,
                )
                for pair in range(2):
                    both = four[:, pair * LANES : (pair + 1) * LANES]
                    slot = 4 * quad + 2 * pair
                    top, bottom = both[: FEAT // 2], both[FEAT // 2 :]
                    feat_out[slot] = jnp.where(left, top, pltpu.roll(bottom, HALF, 1)).astype(jnp.bfloat16)
                    feat_out[slot + 1] = jnp.where(left, pltpu.roll(top, HALF, 1), bottom).astype(jnp.bfloat16)
            send(1 + ITERS, lambda to: feat_out.at[to], feat_in.at[me], recv_sem.at[1 + ITERS])

        arrived(1 + iteration, parts.at[iteration])
        col_sum = jnp.sum(parts[iteration].astype(jnp.float32), axis=0)
        scale[...] = mdl_mass_ref[...] / col_sum
        if iteration < ITERS - 1:
            low = scale[...].astype(jnp.bfloat16).astype(jnp.float32)
            col_low = [jnp.broadcast_to(low[line : line + 1], (block, LANES)) for line in range(lines)]

    col_line = jnp.concatenate([scale[line : line + 1, :] for line in range(lines)], axis=1)
    weighted = (model[...].astype(jnp.float32) * col_line).astype(jnp.bfloat16)
    image_terms = lax.dot_general(
        weighted, kern[...], (((1,), (1,)), ((), ())), preferred_element_type=jnp.float32
    )
    grad_img_ref[...] = -(image_terms * row_line)

    feat_in[me] = feat_out[me]
    arrived(1 + ITERS, feat_in)
    summed = jnp.sum(feat_in[...].astype(jnp.float32), axis=0)
    line = scale[pl.ds(me // 2, 1), :]
    even = lax.rem(me, 2) == 0
    own_scale = jnp.where(left[:1] == even, line, pltpu.roll(line, HALF, 1))
    packed = -(summed * own_scale)
    grad_mdl_ref[: FEAT // 2] = packed[:, :HALF]
    grad_mdl_ref[FEAT // 2 :] = pltpu.roll(packed, HALF, 1)[:, :HALF]

    sent(0, units)
    for iteration in range(ITERS):
        sent(1 + iteration, parts.at[iteration])
    sent(1 + ITERS, feat_out)


def store_kernel(grad_img_ref, grad_mdl_ref, grad_img_hbm, grad_mdl_hbm, sems):
    stores = [
        pltpu.make_async_copy(grad_img_ref, grad_img_hbm, sems.at[0]),
        pltpu.make_async_copy(grad_mdl_ref, grad_mdl_hbm, sems.at[1]),
    ]
    for store in stores:
        store.start()
    for store in stores:
        store.wait()


def shards(n, img_feat, mdl_feat, img_mass, mdl_mass):
    rows = img_feat.shape[1]
    share = mdl_feat.shape[1]
    total = share * n
    assert share == HALF and img_feat.shape[0] == FEAT
    lines = total // LANES
    vmem = pl.BlockSpec(memory_space=pltpu.VMEM)
    packed = (n, FEAT // 2, LANES)
    anywhere = pl.BlockSpec(memory_space=pl.ANY)
    grads = pl.pallas_call(
        functools.partial(whole_kernel, n),
        out_shape=(
            pltpu.VMEM((FEAT, rows), jnp.float32),
            pltpu.VMEM((FEAT, share), jnp.float32),
        ),
        in_specs=[pl.BlockSpec(memory_space=pltpu.HBM)] * 4,
        out_specs=(vmem, vmem),
        scratch_shapes=[
            pltpu.VMEM((FEAT, rows), jnp.bfloat16),
            pltpu.VMEM((FEAT, share), jnp.bfloat16),
            pltpu.VMEM((1, rows), jnp.float32),
            pltpu.VMEM((lines, LANES), jnp.float32),
            pltpu.VMEM(packed, jnp.bfloat16),
            pltpu.VMEM((FEAT, total), jnp.bfloat16),
            pltpu.VMEM((rows, total), jnp.bfloat16),
            pltpu.VMEM((rows, total), jnp.float32),
            pltpu.VMEM((rows, LANES), jnp.float32),
            pltpu.VMEM((ITERS, n, lines, LANES), jnp.bfloat16),
            pltpu.VMEM((lines, LANES), jnp.float32),
            pltpu.VMEM(packed, jnp.bfloat16),
            pltpu.VMEM(packed, jnp.bfloat16),
            pltpu.SemaphoreType.DMA((4,)),
            pltpu.SemaphoreType.DMA((n,)),
            pltpu.SemaphoreType.DMA((2 + ITERS,)),
            pltpu.SemaphoreType.DMA((2 + ITERS,)),
        ],
        compiler_params=pltpu.CompilerParams(
            collective_id=0, has_side_effects=True, vmem_limit_bytes=60 * 2**20
        ),
        name="sinkhorn",
    )(img_feat, mdl_feat, img_mass.reshape(1, rows), mdl_mass.reshape(lines, LANES))
    return pl.pallas_call(
        store_kernel,
        out_shape=(
            jax.ShapeDtypeStruct((FEAT, rows), jnp.float32),
            jax.ShapeDtypeStruct((FEAT, share), jnp.float32),
        ),
        in_specs=[vmem] * 2,
        out_specs=(anywhere, anywhere),
        scratch_shapes=[pltpu.SemaphoreType.DMA((2,))],
        compiler_params=pltpu.CompilerParams(vmem_limit_bytes=2**20),
        name="store",
    )(*grads)


def solution(mesh):
    placed = (P(None, ("fish", "img")), P(None, ("fish", "img")), P(("fish", "img")), P("fish"))
    return jax.shard_map(
        functools.partial(shards, mesh.shape["img"]),
        mesh=mesh,
        in_specs=placed,
        out_specs=(P(None, ("fish", "img")), P(None, ("fish", "img"))),
        check_vma=False,
    )
```

```python
import functools

import jax
import jax.numpy as jnp
from jax import lax
from jax.experimental import pallas as pl
from jax.experimental.pallas import tpu as pltpu
from jax.sharding import PartitionSpec as P

FEAT = 64
ITERS = 4
LANES = 128
HALF = 64

inv_temp = 20.0


def normalize(features):
    wide = features.astype(jnp.float32)
    guarded = jnp.mean(wide * wide, axis=0, keepdims=True) + 1e-06
    return wide * lax.rsqrt(guarded)


def repeat(count, body, carry=0):
    if count <= 16:
        for step in range(count):
            carry = body(step, carry)
        return carry
    return lax.fori_loop(0, count, body, carry)


def other(index, step, count):
    if not isinstance(step, int) or count & (count - 1):
        return lax.rem(index + step, count)
    bit = 1
    while bit <= step:
        if step & bit:
            index = index + bit * (1 - 2 * lax.rem(index // bit, 2))
        bit *= 2
    return index


def whole_kernel(
    n, img_hbm, mdl_hbm, img_mass_hbm, mdl_mass_hbm, grad_img_ref, grad_mdl_ref,
    img_ref, mdl_ref, img_mass_ref, mdl_mass_ref,
    units, model, kern, wide, row_scale, parts, scale, feat_out, feat_in, load_sem, unit_sem, send_sem, recv_sem,
):
    me = lax.axis_index("img")
    total = kern.shape[1]
    lines = total // LANES

    partners = [other(me, n - 1 - step, n) for step in range(n - 1)] if n <= 16 else None

    def partner(step):
        return partners[step] if partners else other(me, step + 1, n)

    def send(phase, source, target_slot, landed):
        def one(step, carry):
            to = partner(step)
            pltpu.make_async_remote_copy(
                src_ref=source(to),
                dst_ref=target_slot,
                send_sem=send_sem.at[phase],
                recv_sem=landed,
                device_id={"img": to},
                device_id_type=pl.DeviceIdType.MESH,
            ).start()
            return carry

        repeat(n - 1, one)

    def arrived(phase, slots):
        all_but_own = slots.at[pl.ds(0, n - 1)]
        pltpu.make_async_copy(all_but_own, all_but_own, recv_sem.at[phase]).wait()

    def sent(phase, slots):
        all_but_own = slots.at[pl.ds(0, n - 1)]
        pltpu.make_async_copy(all_but_own, all_but_own, send_sem.at[phase]).wait()

    barrier = pltpu.get_barrier_semaphore()

    def greet(step, carry):
        pl.semaphore_signal(
            barrier, inc=1, device_id={"img": partner(step)}, device_id_type=pl.DeviceIdType.MESH
        )
        return carry

    loads = [
        pltpu.make_async_copy(source, target, load_sem.at[slot])
        for slot, (source, target) in enumerate(
            ((mdl_hbm, mdl_ref), (img_hbm, img_ref), (img_mass_hbm, img_mass_ref), (mdl_mass_hbm, mdl_mass_ref))
        )
    ]
    for load in loads:
        load.start()
    repeat(n - 1, greet)
    loads[0].wait()

    own = normalize(mdl_ref[...])
    units[me] = jnp.concatenate([own[: FEAT // 2], own[FEAT // 2 :]], axis=1).astype(jnp.bfloat16)
    pl.semaphore_wait(barrier, n - 1)
    send(0, lambda to: units.at[me], units.at[me], unit_sem.at[me])

    for load in loads[1:]:
        load.wait()
    img_unit = normalize(img_ref[...]).astype(jnp.bfloat16)
    img_rows = img_unit.astype(jnp.float32).T.astype(jnp.bfloat16)
    img_mass = jnp.broadcast_to(img_mass_ref[...], (LANES, img_rows.shape[0])).T
    left = lax.broadcasted_iota(jnp.int32, (FEAT // 2, LANES), 1) < HALF

    factor = inv_temp / FEAT
    chunk = 2 * LANES
    group = chunk // HALF
    rows = kern.shape[0]
    block = 64

    def build(step, carry):
        which = other(me // group, step, n // group)
        for sub in range(group):
            sender = which * group + sub

            @pl.when(sender != me)
            def _():
                pltpu.make_async_copy(units.at[sender], units.at[sender], unit_sem.at[sender]).wait()

        blocks = []
        for sub in range(0, group, 2):
            one = units[which * group + sub].astype(jnp.float32)
            two = units[which * group + sub + 1].astype(jnp.float32)
            top = jnp.where(left, one, pltpu.roll(two, HALF, 1))
            bottom = jnp.where(left, pltpu.roll(one, HALF, 1), two)
            blocks.append(jnp.concatenate([top, bottom], axis=0))
        columns = jnp.concatenate(blocks, axis=1).astype(jnp.bfloat16)
        where = pl.ds(pl.multiple_of(which * chunk, chunk), chunk)
        model[:, where] = columns
        scores = jnp.dot(img_rows, columns, preferred_element_type=jnp.float32)
        tile = jnp.exp(scores * factor).astype(jnp.bfloat16)
        kern[:, where] = tile
        wide[:, where] = tile.astype(jnp.float32)
        return carry

    lax.fori_loop(0, total // chunk, build, 0)
    scale[...] = jnp.ones((lines, LANES), jnp.float32)

    def finish(iteration):
        arrived(1 + iteration, parts.at[iteration])
        col_sum = jnp.sum(parts[iteration].astype(jnp.float32), axis=0)
        scale[...] = mdl_mass_ref[...] / col_sum

    def iterate(iteration, carry):
        @pl.when(iteration > 0)
        def _():
            finish(iteration - 1)

        low = scale[...].astype(jnp.bfloat16).astype(jnp.float32)
        col_low = [jnp.broadcast_to(low[line : line + 1], (block, LANES)) for line in range(lines)]
        partial_cols = jnp.zeros((8, total), jnp.float32)
        for start in range(0, rows, block):
            here = slice(start, start + block)
            by_lane = wide[here, :LANES] * col_low[0]
            for line in range(1, lines):
                by_lane += wide[here, line * LANES : (line + 1) * LANES] * col_low[line]
            scaled = img_mass[here] / jnp.broadcast_to(jnp.sum(by_lane, axis=1, keepdims=True), (block, LANES))
            row_scale[here] = scaled
            row_low = scaled.astype(jnp.bfloat16).astype(jnp.float32)
            row_low = jnp.concatenate([row_low] * lines, axis=1)
            partial_cols += jnp.sum((wide[here] * row_low).reshape(block // 8, 8, total), axis=0)
        partial_cols = jnp.sum(partial_cols, axis=0, keepdims=True)
        for line in range(lines):
            scale[line : line + 1, :] = partial_cols[:, line * LANES : (line + 1) * LANES]
        parts[iteration, me] = scale[...].astype(jnp.bfloat16)
        mine = parts.at[iteration, me]
        send(1 + iteration, lambda to: mine, mine, recv_sem.at[1 + iteration])
        return carry

    lax.fori_loop(0, ITERS, iterate, 0)

    row_line = row_scale[...].T[:1]
    row_feat = (img_unit.astype(jnp.float32) * row_line).astype(jnp.bfloat16)
    for quad in range(n // 4):
        four = jnp.dot(
            row_feat, kern[:, quad * chunk : (quad + 1) * chunk],
            preferred_element_type=jnp.float32,
        )
        for pair in range(2):
            both = four[:, pair * LANES : (pair + 1) * LANES]
            slot = 4 * quad + 2 * pair
            top, bottom = both[: FEAT // 2], both[FEAT // 2 :]
            feat_out[slot] = jnp.where(left, top, pltpu.roll(bottom, HALF, 1)).astype(jnp.bfloat16)
            feat_out[slot + 1] = jnp.where(left, pltpu.roll(top, HALF, 1), bottom).astype(jnp.bfloat16)
    send(1 + ITERS, lambda to: feat_out.at[to], feat_in.at[me], recv_sem.at[1 + ITERS])

    finish(ITERS - 1)
    col_line = jnp.concatenate([scale[line : line + 1, :] for line in range(lines)], axis=1)
    weighted = (model[...].astype(jnp.float32) * col_line).astype(jnp.bfloat16)
    image_terms = lax.dot_general(
        weighted, kern[...], (((1,), (1,)), ((), ())), preferred_element_type=jnp.float32
    )
    grad_img_ref[...] = -(image_terms * row_line)

    feat_in[me] = feat_out[me]
    arrived(1 + ITERS, feat_in)
    summed = jnp.sum(feat_in[...].astype(jnp.float32), axis=0)
    line = scale[pl.ds(me // 2, 1), :]
    even = lax.rem(me, 2) == 0
    own_scale = jnp.where(left[:1] == even, line, pltpu.roll(line, HALF, 1))
    packed = -(summed * own_scale)
    grad_mdl_ref[: FEAT // 2] = packed[:, :HALF]
    grad_mdl_ref[FEAT // 2 :] = pltpu.roll(packed, HALF, 1)[:, :HALF]

    sent(0, units)
    for iteration in range(ITERS):
        sent(1 + iteration, parts.at[iteration])
    sent(1 + ITERS, feat_out)


def store_kernel(grad_img_ref, grad_mdl_ref, grad_img_hbm, grad_mdl_hbm, sems):
    stores = [
        pltpu.make_async_copy(grad_img_ref, grad_img_hbm, sems.at[0]),
        pltpu.make_async_copy(grad_mdl_ref, grad_mdl_hbm, sems.at[1]),
    ]
    for store in stores:
        store.start()
    for store in stores:
        store.wait()


def shards(n, img_feat, mdl_feat, img_mass, mdl_mass):
    rows = img_feat.shape[1]
    share = mdl_feat.shape[1]
    total = share * n
    assert share == HALF and img_feat.shape[0] == FEAT
    lines = total // LANES
    vmem = pl.BlockSpec(memory_space=pltpu.VMEM)
    packed = (n, FEAT // 2, LANES)
    anywhere = pl.BlockSpec(memory_space=pl.ANY)
    grads = pl.pallas_call(
        functools.partial(whole_kernel, n),
        out_shape=(
            pltpu.VMEM((FEAT, rows), jnp.float32),
            pltpu.VMEM((FEAT, share), jnp.float32),
        ),
        in_specs=[pl.BlockSpec(memory_space=pltpu.HBM)] * 4,
        out_specs=(vmem, vmem),
        scratch_shapes=[
            pltpu.VMEM((FEAT, rows), jnp.bfloat16),
            pltpu.VMEM((FEAT, share), jnp.bfloat16),
            pltpu.VMEM((1, rows), jnp.float32),
            pltpu.VMEM((lines, LANES), jnp.float32),
            pltpu.VMEM(packed, jnp.bfloat16),
            pltpu.VMEM((FEAT, total), jnp.bfloat16),
            pltpu.VMEM((rows, total), jnp.bfloat16),
            pltpu.VMEM((rows, total), jnp.float32),
            pltpu.VMEM((rows, LANES), jnp.float32),
            pltpu.VMEM((ITERS, n, lines, LANES), jnp.bfloat16),
            pltpu.VMEM((lines, LANES), jnp.float32),
            pltpu.VMEM(packed, jnp.bfloat16),
            pltpu.VMEM(packed, jnp.bfloat16),
            pltpu.SemaphoreType.DMA((4,)),
            pltpu.SemaphoreType.DMA((n,)),
            pltpu.SemaphoreType.DMA((2 + ITERS,)),
            pltpu.SemaphoreType.DMA((2 + ITERS,)),
        ],
        compiler_params=pltpu.CompilerParams(
            collective_id=0, has_side_effects=True, vmem_limit_bytes=60 * 2**20
        ),
        name="sinkhorn",
    )(img_feat, mdl_feat, img_mass.reshape(1, rows), mdl_mass.reshape(lines, LANES))
    return pl.pallas_call(
        store_kernel,
        out_shape=(
            jax.ShapeDtypeStruct((FEAT, rows), jnp.float32),
            jax.ShapeDtypeStruct((FEAT, share), jnp.float32),
        ),
        in_specs=[vmem] * 2,
        out_specs=(anywhere, anywhere),
        scratch_shapes=[pltpu.SemaphoreType.DMA((2,))],
        compiler_params=pltpu.CompilerParams(vmem_limit_bytes=2**20),
        name="store",
    )(*grads)


def solution(mesh):
    placed = (P(None, ("fish", "img")), P(None, ("fish", "img")), P(("fish", "img")), P("fish"))
    return jax.shard_map(
        functools.partial(shards, mesh.shape["img"]),
        mesh=mesh,
        in_specs=placed,
        out_specs=(P(None, ("fish", "img")), P(None, ("fish", "img"))),
        check_vma=False,
    )
```

```python
import functools

import jax
import jax.numpy as jnp
from jax import lax
from jax.experimental import pallas as pl
from jax.experimental.pallas import tpu as pltpu
from jax.sharding import PartitionSpec as P

FEAT = 64
ITERS = 4
LANES = 128
HALF = 64

inv_temp = 20.0


def normalize(features):
    wide = features.astype(jnp.float32)
    guarded = jnp.mean(wide * wide, axis=0, keepdims=True) + 1e-06
    return wide * lax.rsqrt(guarded)


def repeat(count, body, carry=0):
    if count <= 16:
        for step in range(count):
            carry = body(step, carry)
        return carry
    return lax.fori_loop(0, count, body, carry)


def other(index, step, count):
    if not isinstance(step, int) or count & (count - 1):
        return lax.rem(index + step, count)
    bit = 1
    while bit <= step:
        if step & bit:
            index = index + bit * (1 - 2 * lax.rem(index // bit, 2))
        bit *= 2
    return index


def whole_kernel(
    n, img_hbm, mdl_hbm, img_mass_hbm, mdl_mass_hbm, grad_img_ref, grad_mdl_ref,
    img_ref, mdl_ref, img_mass_ref, mdl_mass_ref,
    units, model, kern, wide, row_scale, parts, scale, feat_out, feat_in, load_sem, unit_sem, send_sem, recv_sem,
):
    me = lax.axis_index("img")
    total = kern.shape[1]
    lines = total // LANES

    partners = [other(me, n - 1 - step, n) for step in range(n - 1)] if n <= 16 else None

    def partner(step):
        return partners[step] if partners else other(me, step + 1, n)

    def send(phase, source, target_slot, landed):
        def one(step, carry):
            to = partner(step)
            pltpu.make_async_remote_copy(
                src_ref=source(to),
                dst_ref=target_slot,
                send_sem=send_sem.at[phase],
                recv_sem=landed,
                device_id={"img": to},
                device_id_type=pl.DeviceIdType.MESH,
            ).start()
            return carry

        repeat(n - 1, one)

    def arrived(phase, slots):
        all_but_own = slots.at[pl.ds(0, n - 1)]
        pltpu.make_async_copy(all_but_own, all_but_own, recv_sem.at[phase]).wait()

    def sent(phase, slots):
        all_but_own = slots.at[pl.ds(0, n - 1)]
        pltpu.make_async_copy(all_but_own, all_but_own, send_sem.at[phase]).wait()

    barrier = pltpu.get_barrier_semaphore()

    def greet(step, carry):
        pl.semaphore_signal(
            barrier, inc=1, device_id={"img": partner(step)}, device_id_type=pl.DeviceIdType.MESH
        )
        return carry

    loads = [
        pltpu.make_async_copy(source, target, load_sem.at[slot])
        for slot, (source, target) in enumerate(
            ((mdl_hbm, mdl_ref), (img_hbm, img_ref), (img_mass_hbm, img_mass_ref), (mdl_mass_hbm, mdl_mass_ref))
        )
    ]
    for load in loads:
        load.start()
    repeat(n - 1, greet)
    loads[0].wait()

    own = normalize(mdl_ref[...])
    units[me] = jnp.concatenate([own[: FEAT // 2], own[FEAT // 2 :]], axis=1).astype(jnp.bfloat16)
    pl.semaphore_wait(barrier, n - 1)
    send(0, lambda to: units.at[me], units.at[me], unit_sem.at[me])

    for load in loads[1:]:
        load.wait()
    img_unit = normalize(img_ref[...]).astype(jnp.bfloat16)
    img_rows = img_unit.astype(jnp.float32).T.astype(jnp.bfloat16)
    img_mass = jnp.broadcast_to(img_mass_ref[...], (LANES, img_rows.shape[0])).T
    left = lax.broadcasted_iota(jnp.int32, (FEAT // 2, LANES), 1) < HALF

    factor = inv_temp / FEAT
    chunk = 2 * LANES
    group = chunk // HALF
    rows = kern.shape[0]
    block = 16

    def build(step, carry):
        which = other(me // group, step, n // group)
        for sub in range(group):
            sender = which * group + sub

            @pl.when(sender != me)
            def _():
                pltpu.make_async_copy(units.at[sender], units.at[sender], unit_sem.at[sender]).wait()

        blocks = []
        for sub in range(0, group, 2):
            one = units[which * group + sub].astype(jnp.float32)
            two = units[which * group + sub + 1].astype(jnp.float32)
            top = jnp.where(left, one, pltpu.roll(two, HALF, 1))
            bottom = jnp.where(left, pltpu.roll(one, HALF, 1), two)
            blocks.append(jnp.concatenate([top, bottom], axis=0))
        columns = jnp.concatenate(blocks, axis=1).astype(jnp.bfloat16)
        where = pl.ds(pl.multiple_of(which * chunk, chunk), chunk)
        model[:, where] = columns
        scores = jnp.dot(img_rows, columns, preferred_element_type=jnp.float32)
        tile = jnp.exp(scores * factor).astype(jnp.bfloat16)
        kern[:, where] = tile
        wide[:, where] = tile.astype(jnp.float32)
        return carry

    lax.fori_loop(0, total // chunk, build, 0)
    scale[...] = jnp.ones((lines, LANES), jnp.float32)

    def finish(iteration):
        arrived(1 + iteration, parts.at[iteration])
        col_sum = jnp.sum(parts[iteration].astype(jnp.float32), axis=0)
        scale[...] = mdl_mass_ref[...] / col_sum

    def iterate(iteration, carry):
        @pl.when(iteration > 0)
        def _():
            finish(iteration - 1)

        low = scale[...].astype(jnp.bfloat16).astype(jnp.float32)
        col_low = [jnp.broadcast_to(low[line : line + 1], (block, LANES)) for line in range(lines)]
        partial_cols = jnp.zeros((8, total), jnp.float32)
        for start in range(0, rows, block):
            here = slice(start, start + block)
            by_lane = wide[here, :LANES] * col_low[0]
            for line in range(1, lines):
                by_lane += wide[here, line * LANES : (line + 1) * LANES] * col_low[line]
            scaled = img_mass[here] / jnp.broadcast_to(jnp.sum(by_lane, axis=1, keepdims=True), (block, LANES))
            row_scale[here] = scaled
            row_low = scaled.astype(jnp.bfloat16).astype(jnp.float32)
            row_low = jnp.concatenate([row_low] * lines, axis=1)
            partial_cols += jnp.sum((wide[here] * row_low).reshape(block // 8, 8, total), axis=0)
        partial_cols = jnp.sum(partial_cols, axis=0, keepdims=True)
        for line in range(lines):
            scale[line : line + 1, :] = partial_cols[:, line * LANES : (line + 1) * LANES]
        parts[iteration, me] = scale[...].astype(jnp.bfloat16)
        mine = parts.at[iteration, me]
        send(1 + iteration, lambda to: mine, mine, recv_sem.at[1 + iteration])
        return carry

    lax.fori_loop(0, ITERS, iterate, 0)

    row_line = row_scale[...].T[:1]
    row_feat = (img_unit.astype(jnp.float32) * row_line).astype(jnp.bfloat16)
    for quad in range(n // 4):
        four = jnp.dot(
            row_feat, kern[:, quad * chunk : (quad + 1) * chunk],
            preferred_element_type=jnp.float32,
        )
        for pair in range(2):
            both = four[:, pair * LANES : (pair + 1) * LANES]
            slot = 4 * quad + 2 * pair
            top, bottom = both[: FEAT // 2], both[FEAT // 2 :]
            feat_out[slot] = jnp.where(left, top, pltpu.roll(bottom, HALF, 1)).astype(jnp.bfloat16)
            feat_out[slot + 1] = jnp.where(left, pltpu.roll(top, HALF, 1), bottom).astype(jnp.bfloat16)
    send(1 + ITERS, lambda to: feat_out.at[to], feat_in.at[me], recv_sem.at[1 + ITERS])

    finish(ITERS - 1)
    col_line = jnp.concatenate([scale[line : line + 1, :] for line in range(lines)], axis=1)
    weighted = (model[...].astype(jnp.float32) * col_line).astype(jnp.bfloat16)
    image_terms = lax.dot_general(
        weighted, kern[...], (((1,), (1,)), ((), ())), preferred_element_type=jnp.float32
    )
    grad_img_ref[...] = -(image_terms * row_line)

    feat_in[me] = feat_out[me]
    arrived(1 + ITERS, feat_in)
    summed = jnp.sum(feat_in[...].astype(jnp.float32), axis=0)
    line = scale[pl.ds(me // 2, 1), :]
    even = lax.rem(me, 2) == 0
    own_scale = jnp.where(left[:1] == even, line, pltpu.roll(line, HALF, 1))
    packed = -(summed * own_scale)
    grad_mdl_ref[: FEAT // 2] = packed[:, :HALF]
    grad_mdl_ref[FEAT // 2 :] = pltpu.roll(packed, HALF, 1)[:, :HALF]

    sent(0, units)
    for iteration in range(ITERS):
        sent(1 + iteration, parts.at[iteration])
    sent(1 + ITERS, feat_out)


def store_kernel(grad_img_ref, grad_mdl_ref, grad_img_hbm, grad_mdl_hbm, sems):
    stores = [
        pltpu.make_async_copy(grad_img_ref, grad_img_hbm, sems.at[0]),
        pltpu.make_async_copy(grad_mdl_ref, grad_mdl_hbm, sems.at[1]),
    ]
    for store in stores:
        store.start()
    for store in stores:
        store.wait()


def shards(n, img_feat, mdl_feat, img_mass, mdl_mass):
    rows = img_feat.shape[1]
    share = mdl_feat.shape[1]
    total = share * n
    assert share == HALF and img_feat.shape[0] == FEAT
    lines = total // LANES
    vmem = pl.BlockSpec(memory_space=pltpu.VMEM)
    packed = (n, FEAT // 2, LANES)
    anywhere = pl.BlockSpec(memory_space=pl.ANY)
    grads = pl.pallas_call(
        functools.partial(whole_kernel, n),
        out_shape=(
            pltpu.VMEM((FEAT, rows), jnp.float32),
            pltpu.VMEM((FEAT, share), jnp.float32),
        ),
        in_specs=[pl.BlockSpec(memory_space=pltpu.HBM)] * 4,
        out_specs=(vmem, vmem),
        scratch_shapes=[
            pltpu.VMEM((FEAT, rows), jnp.bfloat16),
            pltpu.VMEM((FEAT, share), jnp.bfloat16),
            pltpu.VMEM((1, rows), jnp.float32),
            pltpu.VMEM((lines, LANES), jnp.float32),
            pltpu.VMEM(packed, jnp.bfloat16),
            pltpu.VMEM((FEAT, total), jnp.bfloat16),
            pltpu.VMEM((rows, total), jnp.bfloat16),
            pltpu.VMEM((rows, total), jnp.float32),
            pltpu.VMEM((rows, LANES), jnp.float32),
            pltpu.VMEM((ITERS, n, lines, LANES), jnp.bfloat16),
            pltpu.VMEM((lines, LANES), jnp.float32),
            pltpu.VMEM(packed, jnp.bfloat16),
            pltpu.VMEM(packed, jnp.bfloat16),
            pltpu.SemaphoreType.DMA((4,)),
            pltpu.SemaphoreType.DMA((n,)),
            pltpu.SemaphoreType.DMA((2 + ITERS,)),
            pltpu.SemaphoreType.DMA((2 + ITERS,)),
        ],
        compiler_params=pltpu.CompilerParams(
            collective_id=0, has_side_effects=True, vmem_limit_bytes=60 * 2**20
        ),
        name="sinkhorn",
    )(img_feat, mdl_feat, img_mass.reshape(1, rows), mdl_mass.reshape(lines, LANES))
    return pl.pallas_call(
        store_kernel,
        out_shape=(
            jax.ShapeDtypeStruct((FEAT, rows), jnp.float32),
            jax.ShapeDtypeStruct((FEAT, share), jnp.float32),
        ),
        in_specs=[vmem] * 2,
        out_specs=(anywhere, anywhere),
        scratch_shapes=[pltpu.SemaphoreType.DMA((2,))],
        compiler_params=pltpu.CompilerParams(vmem_limit_bytes=2**20),
        name="store",
    )(*grads)


def solution(mesh):
    placed = (P(None, ("fish", "img")), P(None, ("fish", "img")), P(("fish", "img")), P("fish"))
    return jax.shard_map(
        functools.partial(shards, mesh.shape["img"]),
        mesh=mesh,
        in_specs=placed,
        out_specs=(P(None, ("fish", "img")), P(None, ("fish", "img"))),
        check_vma=False,
    )
```

```python
import functools

import jax
import jax.numpy as jnp
from jax import lax
from jax.experimental import pallas as pl
from jax.experimental.pallas import tpu as pltpu
from jax.sharding import PartitionSpec as P

FEAT = 64
ITERS = 4
LANES = 128
HALF = 64

inv_temp = 20.0


def normalize(features):
    wide = features.astype(jnp.float32)
    guarded = jnp.mean(wide * wide, axis=0, keepdims=True) + 1e-06
    return wide * lax.rsqrt(guarded)


def repeat(count, body, carry=0):
    if count <= 16:
        for step in range(count):
            carry = body(step, carry)
        return carry
    return lax.fori_loop(0, count, body, carry)


def other(index, step, count):
    if not isinstance(step, int) or count & (count - 1):
        return lax.rem(index + step, count)
    bit = 1
    while bit <= step:
        if step & bit:
            index = index + bit * (1 - 2 * lax.rem(index // bit, 2))
        bit *= 2
    return index


def whole_kernel(
    n, img_hbm, mdl_hbm, img_mass_hbm, mdl_mass_hbm, grad_img_ref, grad_mdl_ref,
    img_ref, mdl_ref, img_mass_ref, mdl_mass_ref,
    units, model, kern, wide, row_scale, parts, scale, feat_out, feat_in, load_sem, unit_sem, send_sem, recv_sem,
):
    me = lax.axis_index("img")
    total = kern.shape[1]
    lines = total // LANES

    partners = [other(me, n - 1 - step, n) for step in range(n - 1)] if n <= 16 else None

    def partner(step):
        return partners[step] if partners else other(me, step + 1, n)

    def send(phase, source, target_slot, landed):
        def one(step, carry):
            to = partner(step)
            pltpu.make_async_remote_copy(
                src_ref=source(to),
                dst_ref=target_slot,
                send_sem=send_sem.at[phase],
                recv_sem=landed,
                device_id={"img": to},
                device_id_type=pl.DeviceIdType.MESH,
            ).start()
            return carry

        repeat(n - 1, one)

    def arrived(phase, slots):
        all_but_own = slots.at[pl.ds(0, n - 1)]
        pltpu.make_async_copy(all_but_own, all_but_own, recv_sem.at[phase]).wait()

    def sent(phase, slots):
        all_but_own = slots.at[pl.ds(0, n - 1)]
        pltpu.make_async_copy(all_but_own, all_but_own, send_sem.at[phase]).wait()

    barrier = pltpu.get_barrier_semaphore()

    def greet(step, carry):
        pl.semaphore_signal(
            barrier, inc=1, device_id={"img": partner(step)}, device_id_type=pl.DeviceIdType.MESH
        )
        return carry

    loads = [
        pltpu.make_async_copy(source, target, load_sem.at[slot])
        for slot, (source, target) in enumerate(
            ((mdl_hbm, mdl_ref), (img_hbm, img_ref), (img_mass_hbm, img_mass_ref), (mdl_mass_hbm, mdl_mass_ref))
        )
    ]
    repeat(n - 1, greet)
    for load in loads:
        load.start()
    loads[0].wait()

    own = normalize(mdl_ref[...])
    units[me] = jnp.concatenate([own[: FEAT // 2], own[FEAT // 2 :]], axis=1).astype(jnp.bfloat16)
    pl.semaphore_wait(barrier, n - 1)
    send(0, lambda to: units.at[me], units.at[me], unit_sem.at[me])

    for load in loads[1:]:
        load.wait()
    img_unit = normalize(img_ref[...]).astype(jnp.bfloat16)
    img_rows = img_unit.astype(jnp.float32).T.astype(jnp.bfloat16)
    img_mass = jnp.broadcast_to(img_mass_ref[...], (LANES, img_rows.shape[0])).T
    left = lax.broadcasted_iota(jnp.int32, (FEAT // 2, LANES), 1) < HALF

    factor = inv_temp / FEAT
    chunk = 2 * LANES
    group = chunk // HALF
    rows = kern.shape[0]
    block = 16

    def build(step, carry):
        which = other(me // group, step, n // group)
        for sub in range(group):
            sender = which * group + sub

            @pl.when(sender != me)
            def _():
                pltpu.make_async_copy(units.at[sender], units.at[sender], unit_sem.at[sender]).wait()

        blocks = []
        for sub in range(0, group, 2):
            one = units[which * group + sub].astype(jnp.float32)
            two = units[which * group + sub + 1].astype(jnp.float32)
            top = jnp.where(left, one, pltpu.roll(two, HALF, 1))
            bottom = jnp.where(left, pltpu.roll(one, HALF, 1), two)
            blocks.append(jnp.concatenate([top, bottom], axis=0))
        columns = jnp.concatenate(blocks, axis=1).astype(jnp.bfloat16)
        where = pl.ds(pl.multiple_of(which * chunk, chunk), chunk)
        model[:, where] = columns
        scores = jnp.dot(img_rows, columns, preferred_element_type=jnp.float32)
        tile = jnp.exp(scores * factor).astype(jnp.bfloat16)
        kern[:, where] = tile
        wide[:, where] = tile.astype(jnp.float32)
        return carry

    lax.fori_loop(0, total // chunk, build, 0)
    scale[...] = jnp.ones((lines, LANES), jnp.float32)

    def finish(iteration):
        arrived(1 + iteration, parts.at[iteration])
        col_sum = jnp.sum(parts[iteration], axis=0)
        scale[...] = mdl_mass_ref[...] / col_sum

    def iterate(iteration, carry):
        @pl.when(iteration > 0)
        def _():
            finish(iteration - 1)

        low = scale[...].astype(jnp.bfloat16).astype(jnp.float32)
        col_low = [jnp.broadcast_to(low[line : line + 1], (block, LANES)) for line in range(lines)]
        partial_cols = jnp.zeros((8, total), jnp.float32)
        for start in range(0, rows, block):
            here = slice(start, start + block)
            by_lane = wide[here, :LANES] * col_low[0]
            for line in range(1, lines):
                by_lane += wide[here, line * LANES : (line + 1) * LANES] * col_low[line]
            scaled = img_mass[here] / jnp.broadcast_to(jnp.sum(by_lane, axis=1, keepdims=True), (block, LANES))
            row_scale[here] = scaled
            row_low = scaled.astype(jnp.bfloat16).astype(jnp.float32)
            row_low = jnp.concatenate([row_low] * lines, axis=1)
            partial_cols += jnp.sum((wide[here] * row_low).reshape(block // 8, 8, total), axis=0)
        partial_cols = jnp.sum(partial_cols, axis=0, keepdims=True)
        for line in range(lines):
            parts[iteration, me, line : line + 1, :] = partial_cols[:, line * LANES : (line + 1) * LANES]
        mine = parts.at[iteration, me]
        send(1 + iteration, lambda to: mine, mine, recv_sem.at[1 + iteration])
        return carry

    lax.fori_loop(0, ITERS, iterate, 0)

    row_line = row_scale[...].T[:1]
    row_feat = (img_unit.astype(jnp.float32) * row_line).astype(jnp.bfloat16)
    for quad in range(n // 4):
        four = jnp.dot(
            row_feat, kern[:, quad * chunk : (quad + 1) * chunk],
            preferred_element_type=jnp.float32,
        )
        for pair in range(2):
            both = four[:, pair * LANES : (pair + 1) * LANES]
            slot = 4 * quad + 2 * pair
            top, bottom = both[: FEAT // 2], both[FEAT // 2 :]
            feat_out[slot] = jnp.where(left, top, pltpu.roll(bottom, HALF, 1)).astype(jnp.bfloat16)
            feat_out[slot + 1] = jnp.where(left, pltpu.roll(top, HALF, 1), bottom).astype(jnp.bfloat16)
    send(1 + ITERS, lambda to: feat_out.at[to], feat_in.at[me], recv_sem.at[1 + ITERS])

    finish(ITERS - 1)
    col_line = jnp.concatenate([scale[line : line + 1, :] for line in range(lines)], axis=1)
    weighted = (model[...].astype(jnp.float32) * col_line).astype(jnp.bfloat16)
    image_terms = lax.dot_general(
        weighted, kern[...], (((1,), (1,)), ((), ())), preferred_element_type=jnp.float32
    )
    grad_img_ref[...] = -(image_terms * row_line)

    feat_in[me] = feat_out[me]
    arrived(1 + ITERS, feat_in)
    summed = jnp.sum(feat_in[...].astype(jnp.float32), axis=0)
    line = scale[pl.ds(me // 2, 1), :]
    even = lax.rem(me, 2) == 0
    own_scale = jnp.where(left[:1] == even, line, pltpu.roll(line, HALF, 1))
    packed = -(summed * own_scale)
    grad_mdl_ref[: FEAT // 2] = packed[:, :HALF]
    grad_mdl_ref[FEAT // 2 :] = pltpu.roll(packed, HALF, 1)[:, :HALF]

    sent(0, units)
    for iteration in range(ITERS):
        sent(1 + iteration, parts.at[iteration])
    sent(1 + ITERS, feat_out)


def store_kernel(grad_img_ref, grad_mdl_ref, grad_img_hbm, grad_mdl_hbm, sems):
    stores = [
        pltpu.make_async_copy(grad_img_ref, grad_img_hbm, sems.at[0]),
        pltpu.make_async_copy(grad_mdl_ref, grad_mdl_hbm, sems.at[1]),
    ]
    for store in stores:
        store.start()
    for store in stores:
        store.wait()


def shards(n, img_feat, mdl_feat, img_mass, mdl_mass):
    rows = img_feat.shape[1]
    share = mdl_feat.shape[1]
    total = share * n
    assert share == HALF and img_feat.shape[0] == FEAT
    lines = total // LANES
    vmem = pl.BlockSpec(memory_space=pltpu.VMEM)
    packed = (n, FEAT // 2, LANES)
    anywhere = pl.BlockSpec(memory_space=pl.ANY)
    grads = pl.pallas_call(
        functools.partial(whole_kernel, n),
        out_shape=(
            pltpu.VMEM((FEAT, rows), jnp.float32),
            pltpu.VMEM((FEAT, share), jnp.float32),
        ),
        in_specs=[pl.BlockSpec(memory_space=pltpu.HBM)] * 4,
        out_specs=(vmem, vmem),
        scratch_shapes=[
            pltpu.VMEM((FEAT, rows), jnp.bfloat16),
            pltpu.VMEM((FEAT, share), jnp.bfloat16),
            pltpu.VMEM((1, rows), jnp.float32),
            pltpu.VMEM((lines, LANES), jnp.float32),
            pltpu.VMEM(packed, jnp.bfloat16),
            pltpu.VMEM((FEAT, total), jnp.bfloat16),
            pltpu.VMEM((rows, total), jnp.bfloat16),
            pltpu.VMEM((rows, total), jnp.float32),
            pltpu.VMEM((rows, LANES), jnp.float32),
            pltpu.VMEM((ITERS, n, lines, LANES), jnp.float32),
            pltpu.VMEM((lines, LANES), jnp.float32),
            pltpu.VMEM(packed, jnp.bfloat16),
            pltpu.VMEM(packed, jnp.bfloat16),
            pltpu.SemaphoreType.DMA((4,)),
            pltpu.SemaphoreType.DMA((n,)),
            pltpu.SemaphoreType.DMA((2 + ITERS,)),
            pltpu.SemaphoreType.DMA((2 + ITERS,)),
        ],
        compiler_params=pltpu.CompilerParams(
            collective_id=0, has_side_effects=True, vmem_limit_bytes=60 * 2**20
        ),
        name="sinkhorn",
    )(img_feat, mdl_feat, img_mass.reshape(1, rows), mdl_mass.reshape(lines, LANES))
    return pl.pallas_call(
        store_kernel,
        out_shape=(
            jax.ShapeDtypeStruct((FEAT, rows), jnp.float32),
            jax.ShapeDtypeStruct((FEAT, share), jnp.float32),
        ),
        in_specs=[vmem] * 2,
        out_specs=(anywhere, anywhere),
        scratch_shapes=[pltpu.SemaphoreType.DMA((2,))],
        compiler_params=pltpu.CompilerParams(vmem_limit_bytes=2**20),
        name="store",
    )(*grads)


def solution(mesh):
    placed = (P(None, ("fish", "img")), P(None, ("fish", "img")), P(("fish", "img")), P("fish"))
    return jax.shard_map(
        functools.partial(shards, mesh.shape["img"]),
        mesh=mesh,
        in_specs=placed,
        out_specs=(P(None, ("fish", "img")), P(None, ("fish", "img"))),
        check_vma=False,
    )
```
